32 devices in a mesh: seq: 16 (over z, x, core), chan: 2 (over y).
Axes of the slice: x: 2, y: 2, z: 4, core: 2. Of those that a mesh axis runs over, the one named last changes fastest.
Arguments:
- q_gate: float32 [8192, 2048], P('seq', 'chan'), may hold values from -6 to 6
- k_gate: float32 [8192, 2048], P('seq', 'chan'), may hold values from -6 to 6
- values: float32 [8192, 2048], P('seq', 'chan'), may hold values from -6 to 6
- filter_raw: float32 [8192, 128], P('seq'), may hold values from -6 to 6
- grad_out: float32 [8192, 2048], P('seq', 'chan'), may hold values from -6 to 6
Outputs:
- grad_q: float32 [8192, 2048], P('seq', 'chan')
- grad_k: float32 [8192, 2048], P('seq', 'chan')
- grad_v: float32 [8192, 2048], P('seq', 'chan')
- grad_filter: float32 [8192, 128], P('seq')
The draws below stay inside these ranges and needn't reach their ends.
All inputs are finite; a program needn't handle non-finite values.
Results may differ from the reference program's by a relative error of at most 0.0001.
Values sent between devices are 32-bit elements; how exact they have to be, the bound alone decides.
A program may use at most 128 MiB of HBM per device.

```python
import jax
import jax.numpy as jnp

C = 2048
FILTERS = 128
LENGTH = 8192


def steps_of(own_key, dims, shards, low, top_value):
    level = 1.0
    for dim, shards_of in shards:
        steps = jax.random.uniform(jax.random.fold_in(jax.random.fold_in(own_key, 6), dim), (shards_of,), jnp.float32, low / len(shards), top_value / len(shards))
        level = level * jnp.repeat(jnp.exp(steps), dims[dim] // shards_of).reshape((-1,) + (1,) * (len(dims) - 1 - dim))
    return level


def noise(key, dims, spread, limit, pieces=(), held_as=jnp.bfloat16):
    array = spread * jax.random.normal(key, dims, jnp.float32)
    if pieces:
        array = array * steps_of(key, dims, pieces, -0.22, 0.18)
    return jnp.clip(array, -limit, limit).astype(held_as)


def setup_inputs(seed: int = 0) -> dict:
    key_of = jax.random.split(jax.random.key(seed), 6)
    q_gate = noise(key_of[0], (LENGTH, C), 1.0, 6.0, ((0, 16), (1, 2)), jnp.float32)
    k_gate = noise(key_of[1], (LENGTH, C), 1.0, 6.0, ((0, 16), (1, 2)), jnp.float32)
    values = noise(key_of[2], (LENGTH, C), 1.0, 6.0, ((0, 16), (1, 2)), jnp.float32)
    filter_raw = noise(key_of[3], (LENGTH, FILTERS), 1.0, 6.0, ((0, 16),), jnp.float32)
    grad_out = noise(key_of[4], (LENGTH, C), 1.0, 6.0, ((0, 16), (1, 2)), jnp.float32)
    return dict(q_gate=q_gate, k_gate=k_gate, values=values, filter_raw=filter_raw, grad_out=grad_out)


def reference(q_gate, k_gate, values, filter_raw, grad_out):
    length = q_gate.shape[0]
    total = 2 * length
    scale = length ** -0.5
    filt = jnp.tile(filter_raw, (1, C // FILTERS)) * scale
    gated = k_gate * values
    grad_conv = grad_out * q_gate
    spec_gated = jnp.fft.rfft(gated, n=total, axis=0)
    spec_filt = jnp.fft.rfft(filt, n=total, axis=0)
    spec_grad = jnp.fft.rfft(grad_conv, n=total, axis=0)
    conv = jnp.fft.irfft(spec_filt * spec_gated, n=total, axis=0)[:length]
    grad_gated = jnp.fft.irfft(jnp.conj(spec_filt) * spec_grad, n=total, axis=0)[:length]
    corr = jnp.fft.irfft(jnp.conj(spec_gated) * spec_grad, n=total, axis=0)[:length]
    grad_filter = scale * jnp.sum(corr.reshape(length, C // FILTERS, FILTERS), axis=1)
    grad_q = grad_out * conv
    grad_k = grad_gated * values
    grad_v = grad_gated * k_gate
    return (grad_q.astype(jnp.float32), grad_k.astype(jnp.float32),
            grad_v.astype(jnp.float32), grad_filter.astype(jnp.float32))
```

```python
import jax
import jax.numpy as jnp
import numpy as np
from jax import lax
from jax.sharding import PartitionSpec as P

FINE = 128


def mul(form, left, right):
    return jnp.einsum(form, left, right, precision=lax.Precision.HIGH)


def tables(length):
    n1 = length // FINE
    k = np.arange(n1) + 0.25
    coarse = 2.0 * np.pi * np.outer(k, np.arange(n1)) / n1
    first = np.stack([np.cos(coarse), -np.sin(coarse)])
    last = np.stack([np.cos(coarse), -np.sin(coarse)]) / length
    twist = 2.0 * np.pi * np.outer(k, np.arange(FINE)) / length
    fine = 2.0 * np.pi * (np.outer(np.arange(FINE), np.arange(FINE)) % FINE) / FINE
    cos, sin = np.cos(fine), np.sin(fine)
    ahead = np.stack([np.stack([cos, sin]), np.stack([-sin, cos])])
    back = np.stack([np.stack([cos, -sin]), np.stack([sin, cos])])
    return [np.asarray(t, np.float32) for t in (first, last, np.cos(twist), np.sin(twist), ahead, back)]


def local(q_gate, k_gate, values, filter_raw, grad_out):
    rows, width = q_gate.shape
    nfilt = filter_raw.shape[1]
    shards = lax.axis_size("seq")
    length = rows * shards
    repeats = width // nfilt
    own = nfilt // shards
    chans = repeats * own
    scale = float(length) ** (-0.5)
    n1 = length // FINE
    first, last, tw_cos, tw_sin, ahead, back = tables(length)
    tw_cos = tw_cos[None, :, :, None][0]
    tw_sin = tw_sin[None, :, :, None][0]

    def split(block):
        groups = block.shape[1] // nfilt
        parts = block.reshape(rows, groups, shards, own)
        return parts.transpose(2, 0, 1, 3).reshape(shards, rows, groups * own)

    def merge(parts):
        groups = parts.shape[2] // own
        block = parts.reshape(shards, rows, groups, own).transpose(1, 2, 0, 3)
        return block.reshape(rows, groups * nfilt)

    def exchange(parts):
        return lax.all_to_all(parts, "seq", split_axis=0, concat_axis=0, tiled=True)

    def forward(block):
        wide = block.shape[1]
        part = mul("pkn,nbw->pkbw", first, block.reshape(n1, FINE, wide))
        real, imag = part[0], part[1]
        turned = jnp.stack([real * tw_cos + imag * tw_sin, imag * tw_cos - real * tw_sin])
        return mul("opkn,ptnw->otkw", ahead, turned)

    def inverse(spec):
        wide = spec.shape[3]
        part = mul("opkn,ptnw->otkw", back, spec)
        real, imag = part[0], part[1]
        turned = jnp.stack([real * tw_cos - imag * tw_sin, imag * tw_cos + real * tw_sin])
        return mul("pkn,pkbw->nbw", last, turned).reshape(length, wide)

    pair = jnp.concatenate([split(k_gate * values), split(grad_out * q_gate)], axis=2)
    pair = exchange(pair).reshape(length, 2 * chans)
    filt = split(filter_raw * scale).reshape(shards, -1, FINE)
    filt = exchange(filt).reshape(length, own)

    spec = forward(pair)
    gr, gi = spec[0, :, :, :chans], spec[1, :, :, :chans]
    qr, qi = spec[0, :, :, chans:], spec[1, :, :, chans:]
    fspec = jnp.tile(forward(filt), (1, 1, 1, repeats))
    fr, fi = fspec[0], fspec[1]
    conv = jnp.stack([fr * gr - fi * gi, fr * gi + fi * gr])
    adj = jnp.stack([fr * qr + fi * qi, fr * qi - fi * qr])
    corr = jnp.stack([gr * qr + gi * qi, gr * qi - gi * qr])
    corr = corr.reshape(2, n1, FINE, repeats, own).sum(axis=3)
    out = inverse(jnp.concatenate([conv, adj], axis=3)).reshape(shards, rows, 2 * chans)
    lags = inverse(corr).reshape(shards, -1, FINE)
    out = exchange(out)
    lags = exchange(lax.psum(lags, "chan") * scale).reshape(shards, rows, own)

    grad_gated = merge(out[:, :, chans:])
    return (
        grad_out * merge(out[:, :, :chans]),
        grad_gated * values,
        grad_gated * k_gate,
        merge(lags),
    )


def solution(mesh):
    placed = P("seq", "chan")
    return jax.shard_map(
        local,
        mesh=mesh,
        in_specs=(placed, placed, placed, P("seq", None), placed),
        out_specs=(placed, placed, placed, P("seq", None)),
        check_vma=False,
    )
```

```python
import jax
import jax.numpy as jnp
import numpy as np
from jax import lax
from jax.experimental import pallas as pl
from jax.experimental.pallas import tpu as pltpu
from jax.sharding import PartitionSpec as P

FINE = 128


def mul(form, left, right):
    return jnp.einsum(form, left, right, precision=lax.Precision.HIGH)


def tables(length):
    n1 = length // FINE
    k = np.arange(n1) + 0.25
    coarse = 2.0 * np.pi * np.outer(k, np.arange(n1)) / n1
    first = np.stack([np.cos(coarse), -np.sin(coarse)])
    last = np.stack([np.cos(coarse), -np.sin(coarse)]) / length
    twist = 2.0 * np.pi * np.outer(k, np.arange(FINE)) / length
    fine = 2.0 * np.pi * (np.outer(np.arange(FINE), np.arange(FINE)) % FINE) / FINE
    cos, sin = np.cos(fine), np.sin(fine)
    ahead = np.stack([np.stack([cos, sin]), np.stack([-sin, cos])])
    back = np.stack([np.stack([cos, -sin]), np.stack([sin, cos])])
    return [np.asarray(t, np.float32) for t in (first, last, np.cos(twist), np.sin(twist), ahead, back)]


def halves(table):
    high = table.astype(jnp.bfloat16)
    return high, (table - high.astype(np.float32)).astype(jnp.bfloat16)


def split_value(x):
    high = x.astype(jnp.bfloat16)
    return high, (x - high.astype(jnp.float32)).astype(jnp.bfloat16)


def dot(left, right):
    return jnp.dot(left, right, preferred_element_type=jnp.float32)


def kernel_tables(length):
    n1 = length // FINE
    k = np.arange(n1) + 0.25
    pos = np.arange(n1)[None, :] * FINE + np.arange(FINE)[:, None]
    angle = 2.0 * np.pi * (k[None, :, None] * pos[:, None, :]) / length
    ahead = np.concatenate([np.cos(angle), -np.sin(angle)], axis=1).astype(np.float32)
    back = np.swapaxes(ahead, 1, 2) / np.float32(length)
    ah, al = halves(ahead)
    bh, bl = halves(back)
    first = np.concatenate([ah, al, ah], axis=2)
    last = np.concatenate([bh, bl, bh], axis=2)
    fine = 2.0 * np.pi * (np.outer(np.arange(FINE), np.arange(FINE)) % FINE) / FINE
    cos, sin = np.cos(fine), np.sin(fine)
    fwd = np.block([[cos, sin], [-sin, cos]]).astype(np.float32)
    inv = np.block([[cos, -sin], [sin, cos]]).astype(np.float32)
    return first, last, np.stack(halves(fwd) + halves(inv))


def fold_tables(own, chans):
    spots = FINE // own
    lane = np.arange(FINE)
    spread = np.zeros((spots, FINE, FINE), np.float32)
    fold = np.zeros((spots, FINE, FINE), np.float32)
    for j in range(spots):
        spread[j, own * j + lane % own, lane] = 1.0
        used = lane[:chans]
        fold[j, used, own * j + used % own] = 1.0
    return spread.astype(jnp.bfloat16), fold.astype(jnp.bfloat16)


def order_table(width, nfilt, own):
    repeats, shards = width // nfilt, nfilt // own
    cols = np.arange(width).reshape(repeats, shards, own).transpose(1, 0, 2).reshape(-1)
    table = np.zeros((width, width), np.float32)
    table[cols, np.arange(width)] = 1.0
    return table.astype(jnp.bfloat16)


def low_lanes(rows):
    return lax.broadcasted_iota(jnp.int32, (rows, FINE), 1) < FINE // 2


def pack_kernel(k_ref, v_ref, o_ref, q_ref, table_ref, out_ref):
    table = table_ref[...]
    low = low_lanes(k_ref.shape[0])
    moved = []
    for block in (k_ref[...] * v_ref[...], o_ref[...] * q_ref[...]):
        high, rest = split_value(block)
        moved.append(dot(high, table) + dot(rest, table))
    for j in range(out_ref.shape[0] // 2):
        g, q = (m[:, FINE * j : FINE * (j + 1)] for m in moved)
        out_ref[2 * j] = jnp.where(low, g, pltpu.roll(q, FINE // 2, 1))
        out_ref[2 * j + 1] = jnp.where(low, pltpu.roll(g, FINE // 2, 1), q)


def unpack_kernel(in_ref, k_ref, v_ref, o_ref, table_ref, gq_ref, gk_ref, gv_ref):
    table = table_ref[...]
    low = low_lanes(k_ref.shape[0])
    conv, adj = [], []
    for j in range(in_ref.shape[0] // 2):
        a, b = in_ref[2 * j], in_ref[2 * j + 1]
        conv.append(jnp.where(low, a, pltpu.roll(b, FINE // 2, 1)))
        adj.append(jnp.where(low, pltpu.roll(a, FINE // 2, 1), b))
    moved = []
    for parts in (conv, adj):
        high, rest = split_value(jnp.concatenate(parts, axis=1))
        moved.append(dot(high, table) + dot(rest, table))
    gq_ref[...] = o_ref[...] * moved[0]
    gk_ref[...] = moved[1] * v_ref[...]
    gv_ref[...] = moved[1] * k_ref[...]


def spectral_kernel(
    pair_ref, filt_ref, first_ref, last_ref, fine_ref, spread_ref, fold_ref,
    out_ref, lags_ref, wide_ref, spec_a, spec_b,
):
    length = pair_ref.shape[0]
    n1 = length // FINE
    spots = spread_ref.shape[0]
    short = length // spots

    fh, fl = split_value(filt_ref[...])
    for j in range(spots):
        e = spread_ref[j]
        wide_ref[pl.ds(j, short, stride=spots), :] = dot(fh, e) + dot(fl, e)

    def ahead(n2, carry):
        x = jnp.concatenate(
            [r[pl.ds(n2, n1, stride=FINE), :] for r in (pair_ref, wide_ref)], axis=1
        )
        high, rest = split_value(x)
        y = dot(first_ref[n2], jnp.concatenate([high, high, rest], axis=0))
        spec_a[pl.ds(n2, 2 * n1, stride=FINE), :] = y[:, :FINE]
        spec_b[pl.ds(n2, 2 * n1, stride=FINE), :] = y[:, FINE:]
        return carry

    lax.fori_loop(0, FINE, ahead, 0, unroll=4)

    sign = jnp.where(low_lanes(FINE), 1.0, -1.0)

    def fine(which, re, im):
        high, rest = split_value(jnp.concatenate([re, im], axis=0))
        top, bottom = fine_ref[2 * which], fine_ref[2 * which + 1]
        return dot(top, high) + (dot(bottom, high) + dot(top, rest))

    def middle(k1, carry):
        at_re = pl.ds(pl.multiple_of(k1 * FINE, FINE), FINE)
        at_im = pl.ds(pl.multiple_of((k1 + n1) * FINE, FINE), FINE)
        z = fine(
            0,
            jnp.concatenate([spec_a[at_re, :], spec_b[at_re, :]], axis=1),
            jnp.concatenate([spec_a[at_im, :], spec_b[at_im, :]], axis=1),
        )
        pr, fr = z[:FINE, :FINE], z[:FINE, FINE:]
        pi, fi = z[FINE:, :FINE], z[FINE:, FINE:] * sign
        qr, qi = pltpu.roll(pr, FINE // 2, 1), pltpu.roll(pi, FINE // 2, 1)
        re = jnp.concatenate([fr * pr - fi * pi, pr * qr + pi * qi], axis=1)
        im = jnp.concatenate([fr * pi + fi * pr, pr * qi - pi * qr], axis=1)
        w = fine(1, re, im)
        spec_a[at_re, :] = w[:FINE, :FINE]
        spec_b[at_re, :] = w[:FINE, FINE:]
        spec_a[at_im, :] = w[FINE:, :FINE]
        spec_b[at_im, :] = w[FINE:, FINE:]
        return carry

    lax.fori_loop(0, n1, middle, 0, unroll=2)

    def behind(n2, carry):
        x = jnp.concatenate(
            [r[pl.ds(n2, 2 * n1, stride=FINE), :] for r in (spec_a, spec_b)], axis=1
        )
        high, rest = split_value(x)
        y = dot(last_ref[n2], jnp.concatenate([high, high, rest], axis=0))
        out_ref[pl.ds(n2, n1, stride=FINE), :] = y[:, :FINE]
        wide_ref[pl.ds(n2, n1, stride=FINE), :] = y[:, FINE:]
        return carry

    lax.fori_loop(0, FINE, behind, 0, unroll=4)

    total = jnp.zeros((short, FINE), jnp.float32)
    for j in range(spots):
        high, rest = split_value(wide_ref[pl.ds(j, short, stride=spots), :])
        total += dot(high, fold_ref[j]) + dot(rest, fold_ref[j])
    lags_ref[...] = total


VMEM_BYTES = 60 << 20


def pack(k_gate, values, grad_out, q_gate, shards, table):
    rows, width = k_gate.shape
    tile = 128
    block = pl.BlockSpec((tile, width), lambda i: (i, 0))
    return pl.pallas_call(
        pack_kernel,
        grid=(rows // tile,),
        in_specs=[block] * 4 + [pl.BlockSpec((width, width), lambda i: (0, 0))],
        out_specs=pl.BlockSpec((shards, tile, FINE), lambda i: (0, i, 0)),
        out_shape=jax.ShapeDtypeStruct((shards, rows, FINE), jnp.float32),
        compiler_params=pltpu.CompilerParams(vmem_limit_bytes=VMEM_BYTES),
        cost_estimate=pl.CostEstimate(
            flops=8 * rows * width * width, bytes_accessed=24 * rows * width, transcendentals=0
        ),
        name="pack",
    )(k_gate, values, grad_out, q_gate, table)


def unpack(back, k_gate, values, grad_out, table):
    rows, width = k_gate.shape
    tile = 128
    block = pl.BlockSpec((tile, width), lambda i: (i, 0))
    return pl.pallas_call(
        unpack_kernel,
        grid=(rows // tile,),
        in_specs=[pl.BlockSpec((back.shape[0], tile, FINE), lambda i: (0, i, 0))]
        + [block] * 3
        + [pl.BlockSpec((width, width), lambda i: (0, 0))],
        out_specs=[block] * 3,
        out_shape=[jax.ShapeDtypeStruct((rows, width), jnp.float32)] * 3,
        compiler_params=pltpu.CompilerParams(vmem_limit_bytes=VMEM_BYTES),
        cost_estimate=pl.CostEstimate(
            flops=8 * rows * width * width, bytes_accessed=32 * rows * width, transcendentals=0
        ),
        name="unpack",
    )(back, k_gate, values, grad_out, table)


def spectral(pair, filt, own, chans):
    length = pair.shape[0]
    first, last, fine = kernel_tables(length)
    spread, fold = fold_tables(own, chans)
    return pl.pallas_call(
        spectral_kernel,
        in_specs=[pl.BlockSpec(memory_space=pltpu.VMEM)] * 7,
        out_specs=[pl.BlockSpec(memory_space=pltpu.VMEM)] * 2,
        out_shape=[
            jax.ShapeDtypeStruct(pair.shape, jnp.float32),
            jax.ShapeDtypeStruct(filt.shape, jnp.float32),
        ],
        scratch_shapes=[
            pltpu.VMEM((length, FINE), jnp.float32),
            pltpu.VMEM((2 * length, FINE), jnp.float32),
            pltpu.VMEM((2 * length, FINE), jnp.float32),
        ],
        compiler_params=pltpu.CompilerParams(vmem_limit_bytes=VMEM_BYTES),
        cost_estimate=pl.CostEstimate(
            flops=16_000_000_000, bytes_accessed=24 << 20, transcendentals=0
        ),
        name="spectral",
    )(pair, filt, jnp.asarray(first), jnp.asarray(last), jnp.asarray(fine),
      jnp.asarray(spread), jnp.asarray(fold))


def local(q_gate, k_gate, values, filter_raw, grad_out):
    rows, width = q_gate.shape
    nfilt = filter_raw.shape[1]
    shards = lax.axis_size("seq")
    length = rows * shards
    repeats = width // nfilt
    own = nfilt // shards
    chans = repeats * own
    scale = float(length) ** (-0.5)
    n1 = length // FINE
    first, last, tw_cos, tw_sin, ahead, back = tables(length)
    tw_cos = tw_cos[None, :, :, None][0]
    tw_sin = tw_sin[None, :, :, None][0]

    def split(block):
        groups = block.shape[1] // nfilt
        parts = block.reshape(rows, groups, shards, own)
        return parts.transpose(2, 0, 1, 3).reshape(shards, rows, groups * own)

    def merge(parts):
        groups = parts.shape[2] // own
        block = parts.reshape(shards, rows, groups, own).transpose(1, 2, 0, 3)
        return block.reshape(rows, groups * nfilt)

    def exchange(parts):
        return lax.all_to_all(parts, "seq", split_axis=0, concat_axis=0, tiled=True)

    if 2 * chans == FINE and n1 == 64:
        table = order_table(width, nfilt, own)
        filt = exchange(split(filter_raw * scale).reshape(shards, -1, FINE))
        pair = exchange(pack(k_gate, values, grad_out, q_gate, shards, jnp.asarray(table)))
        out, lags = spectral(
            pair.reshape(length, FINE), filt.reshape(-1, FINE), own, chans
        )
        out = exchange(out.reshape(shards, rows, FINE))
        lags = exchange(lags.reshape(shards, -1, FINE)).reshape(shards, rows, own)
        lags = lax.psum(merge(lags), "chan") * scale
        return tuple(unpack(out, k_gate, values, grad_out, jnp.asarray(table.T))) + (lags,)

    def forward(block):
        wide = block.shape[1]
        part = mul("pkn,nbw->pkbw", first, block.reshape(n1, FINE, wide))
        real, imag = part[0], part[1]
        turned = jnp.stack([real * tw_cos + imag * tw_sin, imag * tw_cos - real * tw_sin])
        return mul("opkn,ptnw->otkw", ahead, turned)

    def inverse(spec):
        wide = spec.shape[3]
        part = mul("opkn,ptnw->otkw", back, spec)
        real, imag = part[0], part[1]
        turned = jnp.stack([real * tw_cos - imag * tw_sin, imag * tw_cos + real * tw_sin])
        return mul("pkn,pkbw->nbw", last, turned).reshape(length, wide)

    pair = jnp.concatenate([split(k_gate * values), split(grad_out * q_gate)], axis=2)
    pair = exchange(pair).reshape(length, 2 * chans)
    filt = split(filter_raw * scale).reshape(shards, -1, FINE)
    filt = exchange(filt).reshape(length, own)

    spec = forward(pair)
    gr, gi = spec[0, :, :, :chans], spec[1, :, :, :chans]
    qr, qi = spec[0, :, :, chans:], spec[1, :, :, chans:]
    fspec = jnp.tile(forward(filt), (1, 1, 1, repeats))
    fr, fi = fspec[0], fspec[1]
    conv = jnp.stack([fr * gr - fi * gi, fr * gi + fi * gr])
    adj = jnp.stack([fr * qr + fi * qi, fr * qi - fi * qr])
    corr = jnp.stack([gr * qr + gi * qi, gr * qi - gi * qr])
    corr = corr.reshape(2, n1, FINE, repeats, own).sum(axis=3)
    out = inverse(jnp.concatenate([conv, adj], axis=3)).reshape(shards, rows, 2 * chans)
    lags = inverse(corr).reshape(shards, -1, FINE)
    out = exchange(out)
    lags = exchange(lax.psum(lags, "chan") * scale).reshape(shards, rows, own)

    grad_gated = merge(out[:, :, chans:])
    return (
        grad_out * merge(out[:, :, :chans]),
        grad_gated * values,
        grad_gated * k_gate,
        merge(lags),
    )


def solution(mesh):
    placed = P("seq", "chan")
    return jax.shard_map(
        local,
        mesh=mesh,
        in_specs=(placed, placed, placed, P("seq", None), placed),
        out_specs=(placed, placed, placed, P("seq", None)),
        check_vma=False,
    )
```

```python
import jax
import jax.numpy as jnp
import numpy as np
from jax import lax
from jax.experimental import pallas as pl
from jax.experimental.pallas import tpu as pltpu
from jax.sharding import PartitionSpec as P

FINE = 128


def mul(form, left, right):
    return jnp.einsum(form, left, right, precision=lax.Precision.HIGH)


def tables(length):
    n1 = length // FINE
    k = np.arange(n1) + 0.25
    coarse = 2.0 * np.pi * np.outer(k, np.arange(n1)) / n1
    first = np.stack([np.cos(coarse), -np.sin(coarse)])
    last = np.stack([np.cos(coarse), -np.sin(coarse)]) / length
    twist = 2.0 * np.pi * np.outer(k, np.arange(FINE)) / length
    fine = 2.0 * np.pi * (np.outer(np.arange(FINE), np.arange(FINE)) % FINE) / FINE
    cos, sin = np.cos(fine), np.sin(fine)
    ahead = np.stack([np.stack([cos, sin]), np.stack([-sin, cos])])
    back = np.stack([np.stack([cos, -sin]), np.stack([sin, cos])])
    return [np.asarray(t, np.float32) for t in (first, last, np.cos(twist), np.sin(twist), ahead, back)]


def halves(table):
    high = table.astype(jnp.bfloat16)
    return high, (table - high.astype(np.float32)).astype(jnp.bfloat16)


def split_value(x):
    high = x.astype(jnp.bfloat16)
    return high, (x - high.astype(jnp.float32)).astype(jnp.bfloat16)


def dot(left, right):
    return jnp.dot(left, right, preferred_element_type=jnp.float32)


def kernel_tables(length):
    n1 = length // FINE
    k = np.arange(n1) + 0.25
    pos = np.arange(n1)[None, :] * FINE + np.arange(FINE)[:, None]
    angle = 2.0 * np.pi * (k[None, :, None] * pos[:, None, :]) / length
    ahead = np.concatenate([np.cos(angle), -np.sin(angle)], axis=1).astype(np.float32)
    back = np.swapaxes(ahead, 1, 2) / np.float32(length)
    ah, al = halves(ahead)
    bh, bl = halves(back)
    first = np.concatenate([ah, al, ah], axis=2)
    last = np.concatenate([bh, bl, bh], axis=2)
    fine = 2.0 * np.pi * (np.outer(np.arange(FINE), np.arange(FINE)) % FINE) / FINE
    cos, sin = np.cos(fine), np.sin(fine)
    fwd = np.block([[cos, sin], [-sin, cos]]).astype(np.float32)
    inv = np.block([[cos, -sin], [sin, cos]]).astype(np.float32)
    return first, last, np.stack(halves(fwd) + halves(inv))


def fold_tables(own, chans):
    spots = FINE // own
    lane = np.arange(FINE)
    spread = np.zeros((spots, FINE, FINE), np.float32)
    fold = np.zeros((spots, FINE, FINE), np.float32)
    for j in range(spots):
        spread[j, own * j + lane % own, lane] = 1.0
        used = lane[:chans]
        fold[j, used, own * j + used % own] = 1.0
    return spread.astype(jnp.bfloat16), fold.astype(jnp.bfloat16)


def order_table(width, nfilt, own):
    repeats, shards = width // nfilt, nfilt // own
    cols = np.arange(width).reshape(repeats, shards, own).transpose(1, 0, 2).reshape(-1)
    table = np.zeros((width, width), np.float32)
    table[cols, np.arange(width)] = 1.0
    return table.astype(jnp.bfloat16)


def low_lanes(rows):
    return lax.broadcasted_iota(jnp.int32, (rows, FINE), 1) < FINE // 2


def pack_kernel(k_ref, v_ref, o_ref, q_ref, table_ref, out_ref):
    table = table_ref[...]
    low = low_lanes(k_ref.shape[0])
    moved = []
    for block in (k_ref[...] * v_ref[...], o_ref[...] * q_ref[...]):
        high, rest = split_value(block)
        moved.append(dot(high, table) + dot(rest, table))
    for j in range(out_ref.shape[0] // 2):
        g, q = (m[:, FINE * j : FINE * (j + 1)] for m in moved)
        out_ref[2 * j] = jnp.where(low, g, pltpu.roll(q, FINE // 2, 1))
        out_ref[2 * j + 1] = jnp.where(low, pltpu.roll(g, FINE // 2, 1), q)


def unpack_kernel(in_ref, k_ref, v_ref, o_ref, table_ref, gq_ref, gk_ref, gv_ref):
    table = table_ref[...]
    low = low_lanes(k_ref.shape[0])
    conv, adj = [], []
    for j in range(in_ref.shape[0] // 2):
        a, b = in_ref[2 * j], in_ref[2 * j + 1]
        conv.append(jnp.where(low, a, pltpu.roll(b, FINE // 2, 1)))
        adj.append(jnp.where(low, pltpu.roll(a, FINE // 2, 1), b))
    moved = []
    for parts in (conv, adj):
        high, rest = split_value(jnp.concatenate(parts, axis=1))
        moved.append(dot(high, table) + dot(rest, table))
    gq_ref[...] = o_ref[...] * moved[0]
    gk_ref[...] = moved[1] * v_ref[...]
    gv_ref[...] = moved[1] * k_ref[...]


STEPS = 8
PITCH = FINE + 8


def fine(fine_ref, which, re, im):
    high, rest = split_value(jnp.concatenate([re, im], axis=0))
    top, bottom = fine_ref[2 * which], fine_ref[2 * which + 1]
    return dot(top, high) + (dot(bottom, high) + dot(top, rest))


def coarse(step, table_ref, src_ref, lines_in, dst_ref, lines_out):
    count = table_ref.shape[0]
    for j in range(count):
        n2 = step * count + j
        high, rest = split_value(src_ref[pl.ds(n2, lines_in, stride=PITCH), :])
        dst_ref[pl.ds(n2, lines_out, stride=PITCH), :] = dot(
            table_ref[j], jnp.concatenate([high, high, rest], axis=0)
        )


def lines(spec_ref, n1, k1):
    at = [pl.multiple_of(p * PITCH, 8) for p in (k1, k1 + n1)]
    return [pl.ds(p, FINE) for p in at]


def filter_kernel(filt_ref, first_ref, fine_ref, spread_ref, out_ref, wide_ref, space_ref, spec_ref):
    i = pl.program_id(0)
    n1 = space_ref.shape[0] // PITCH
    spots = spread_ref.shape[0]
    group = out_ref.shape[1]

    @pl.when(i == 0)
    def _():
        high, rest = split_value(filt_ref[...])
        short = filt_ref.shape[0]
        for j in range(spots):
            e = spread_ref[j]
            wide_ref[pl.ds(j, short, stride=spots), :] = dot(high, e) + dot(rest, e)
        for line in range(n1):
            space_ref[line * PITCH : line * PITCH + FINE, :] = wide_ref[line * FINE : (line + 1) * FINE, :]

    @pl.when(i < STEPS)
    def _():
        coarse(i, first_ref, space_ref, n1, spec_ref, 2 * n1)

    @pl.when(i >= STEPS)
    def _():
        for j in range(group):
            at_re, at_im = lines(spec_ref, n1, (i - STEPS) * group + j)
            z = fine(fine_ref, 0, spec_ref[at_re, :], spec_ref[at_im, :])
            out_ref[0, j] = z[:FINE]
            out_ref[1, j] = z[FINE:]


def main_kernel(pair_ref, fspec_ref, first_ref, last_ref, fine_ref, out_ref, corr_ref, space_ref, spec_ref):
    i = pl.program_id(0)
    n1 = space_ref.shape[0] // PITCH
    group = fspec_ref.shape[1]

    @pl.when(i == 0)
    def _():
        for line in range(n1):
            space_ref[line * PITCH : line * PITCH + FINE, :] = pair_ref[line * FINE : (line + 1) * FINE, :]

    @pl.when(i < STEPS)
    def _():
        coarse(i, first_ref, space_ref, n1, spec_ref, 2 * n1)

    @pl.when((i >= STEPS) & (i < 2 * STEPS))
    def _():
        sign = jnp.where(low_lanes(FINE), 1.0, -1.0)
        for j in range(group):
            at_re, at_im = lines(spec_ref, n1, (i - STEPS) * group + j)
            z = fine(fine_ref, 0, spec_ref[at_re, :], spec_ref[at_im, :])
            pr, pi = z[:FINE], z[FINE:]
            fr, fi = fspec_ref[0, j], fspec_ref[1, j] * sign
            qr, qi = pltpu.roll(pr, FINE // 2, 1), pltpu.roll(pi, FINE // 2, 1)
            corr_ref[0, j] = pr * qr + pi * qi
            corr_ref[1, j] = pr * qi - pi * qr
            w = fine(fine_ref, 1, fr * pr - fi * pi, fr * pi + fi * pr)
            spec_ref[at_re, :] = w[:FINE]
            spec_ref[at_im, :] = w[FINE:]

    @pl.when(i >= 2 * STEPS)
    def _():
        coarse(i - 2 * STEPS, last_ref, spec_ref, 2 * n1, space_ref, n1)

    @pl.when(i == 3 * STEPS - 1)
    def _():
        for line in range(n1):
            out_ref[line * FINE : (line + 1) * FINE, :] = space_ref[line * PITCH : line * PITCH + FINE, :]


def lags_kernel(corr_ref, last_ref, fine_ref, fold_ref, lags_ref, wide_ref, space_ref, spec_ref):
    i = pl.program_id(0)
    n1 = space_ref.shape[0] // PITCH
    spots = fold_ref.shape[0]
    group = corr_ref.shape[1]

    @pl.when(i < STEPS)
    def _():
        for j in range(group):
            at_re, at_im = lines(spec_ref, n1, i * group + j)
            w = fine(fine_ref, 1, corr_ref[0, j], corr_ref[1, j])
            spec_ref[at_re, :] = w[:FINE]
            spec_ref[at_im, :] = w[FINE:]

    @pl.when(i >= STEPS)
    def _():
        coarse(i - STEPS, last_ref, spec_ref, 2 * n1, space_ref, n1)

    @pl.when(i == 2 * STEPS - 1)
    def _():
        for line in range(n1):
            wide_ref[line * FINE : (line + 1) * FINE, :] = space_ref[line * PITCH : line * PITCH + FINE, :]
        short = lags_ref.shape[0]
        total = jnp.zeros((short, FINE), jnp.float32)
        for j in range(spots):
            high, rest = split_value(wide_ref[pl.ds(j, short, stride=spots), :])
            total += dot(high, fold_ref[j]) + dot(rest, fold_ref[j])
        lags_ref[...] = total


VMEM_BYTES = 60 << 20


def pack(k_gate, values, grad_out, q_gate, shards, table):
    rows, width = k_gate.shape
    tile = 128
    block = pl.BlockSpec((tile, width), lambda i: (i, 0))
    return pl.pallas_call(
        pack_kernel,
        grid=(rows // tile,),
        in_specs=[block] * 4 + [pl.BlockSpec((width, width), lambda i: (0, 0))],
        out_specs=pl.BlockSpec((shards, tile, FINE), lambda i: (0, i, 0)),
        out_shape=jax.ShapeDtypeStruct((shards, rows, FINE), jnp.float32),
        compiler_params=pltpu.CompilerParams(vmem_limit_bytes=VMEM_BYTES),
        cost_estimate=pl.CostEstimate(
            flops=8 * rows * width * width, bytes_accessed=24 * rows * width, transcendentals=0
        ),
        name="pack",
    )(k_gate, values, grad_out, q_gate, table)


def unpack(back, k_gate, values, grad_out, table):
    rows, width = k_gate.shape
    tile = 128
    block = pl.BlockSpec((tile, width), lambda i: (i, 0))
    return pl.pallas_call(
        unpack_kernel,
        grid=(rows // tile,),
        in_specs=[pl.BlockSpec((back.shape[0], tile, FINE), lambda i: (0, i, 0))]
        + [block] * 3
        + [pl.BlockSpec((width, width), lambda i: (0, 0))],
        out_specs=[block] * 3,
        out_shape=[jax.ShapeDtypeStruct((rows, width), jnp.float32)] * 3,
        compiler_params=pltpu.CompilerParams(vmem_limit_bytes=VMEM_BYTES),
        cost_estimate=pl.CostEstimate(
            flops=8 * rows * width * width, bytes_accessed=32 * rows * width, transcendentals=0
        ),
        name="unpack",
    )(back, k_gate, values, grad_out, table)


def whole(array):
    return pl.BlockSpec(array.shape, lambda i: (0,) * len(array.shape))


def phase(array, axis, start):
    block = tuple(d // STEPS if a == axis else d for a, d in enumerate(array.shape))

    def index(i):
        at = jnp.clip(i - start, 0, STEPS - 1)
        return tuple(at if a == axis else 0 for a in range(len(block)))

    return pl.BlockSpec(block, index)


def stepped(kernel, phases, ins, in_specs, outs, out_specs, scratch, flops, name):
    return pl.pallas_call(
        kernel,
        grid=(phases * STEPS,),
        in_specs=in_specs,
        out_specs=out_specs,
        out_shape=outs,
        scratch_shapes=[pltpu.VMEM((rows, FINE), jnp.float32) for rows in scratch],
        compiler_params=pltpu.CompilerParams(vmem_limit_bytes=VMEM_BYTES),
        cost_estimate=pl.CostEstimate(
            flops=flops, bytes_accessed=24 << 20, transcendentals=0
        ),
        name=name,
    )(*ins)


def spectral(length, own, chans):
    n1 = length // FINE
    first, last, mats = (jnp.asarray(t) for t in kernel_tables(length))
    spread, fold = (jnp.asarray(t) for t in fold_tables(own, chans))
    spec = jax.ShapeDtypeStruct((2, n1, FINE, FINE), jnp.float32)
    space = jax.ShapeDtypeStruct((length, FINE), jnp.float32)
    packed = jax.ShapeDtypeStruct((length * own // FINE, FINE), jnp.float32)
    padded = [n1 * PITCH, 2 * n1 * PITCH]

    def filter_stage(filt):
        return stepped(
            filter_kernel, 2, (filt, first, mats, spread),
            [whole(filt), phase(first, 0, 0), whole(mats), whole(spread)],
            spec, phase(spec, 1, STEPS), [length] + padded, 15_000_000_000, "filter_spectrum",
        )

    def main_stage(pair, fspec):
        return stepped(
            main_kernel, 3, (pair, fspec, first, last, mats),
            [whole(pair), phase(fspec, 1, STEPS), phase(first, 0, 0), phase(last, 0, 2 * STEPS), whole(mats)],
            [space, spec], [whole(space), phase(spec, 1, STEPS)], padded, 30_000_000_000, "pair_stage",
        )

    def lags_stage(corr):
        return stepped(
            lags_kernel, 2, (corr, last, mats, fold),
            [phase(corr, 1, 0), phase(last, 0, STEPS), whole(mats), whole(fold)],
            packed, whole(packed), [length] + padded, 15_000_000_000, "lags",
        )

    return filter_stage, main_stage, lags_stage


def local(q_gate, k_gate, values, filter_raw, grad_out):
    rows, width = q_gate.shape
    nfilt = filter_raw.shape[1]
    shards = lax.axis_size("seq")
    length = rows * shards
    repeats = width // nfilt
    own = nfilt // shards
    chans = repeats * own
    scale = float(length) ** (-0.5)
    n1 = length // FINE
    first, last, tw_cos, tw_sin, ahead, back = tables(length)
    tw_cos = tw_cos[None, :, :, None][0]
    tw_sin = tw_sin[None, :, :, None][0]

    def split(block):
        groups = block.shape[1] // nfilt
        parts = block.reshape(rows, groups, shards, own)
        return parts.transpose(2, 0, 1, 3).reshape(shards, rows, groups * own)

    def merge(parts):
        groups = parts.shape[2] // own
        block = parts.reshape(shards, rows, groups, own).transpose(1, 2, 0, 3)
        return block.reshape(rows, groups * nfilt)

    def exchange(parts):
        return lax.all_to_all(parts, "seq", split_axis=0, concat_axis=0, tiled=True)

    if 2 * chans == FINE and n1 == 64:
        table = order_table(width, nfilt, own)
        filt = exchange(split(filter_raw * scale).reshape(shards, -1, FINE))
        pair = exchange(pack(k_gate, values, grad_out, q_gate, shards, jnp.asarray(table)))
        filter_stage, main_stage, lags_stage = spectral(length, own, chans)
        fspec = filter_stage(filt.reshape(-1, FINE))
        out, corr = main_stage(pair.reshape(length, FINE), fspec)
        out = exchange(out.reshape(shards, rows, FINE))
        lags = lax.psum(lags_stage(corr), "chan") * scale
        lags = merge(exchange(lags.reshape(shards, -1, FINE)).reshape(shards, rows, own))
        return tuple(unpack(out, k_gate, values, grad_out, jnp.asarray(table.T))) + (lags,)

    def forward(block):
        wide = block.shape[1]
        part = mul("pkn,nbw->pkbw", first, block.reshape(n1, FINE, wide))
        real, imag = part[0], part[1]
        turned = jnp.stack([real * tw_cos + imag * tw_sin, imag * tw_cos - real * tw_sin])
        return mul("opkn,ptnw->otkw", ahead, turned)

    def inverse(spec):
        wide = spec.shape[3]
        part = mul("opkn,ptnw->otkw", back, spec)
        real, imag = part[0], part[1]
        turned = jnp.stack([real * tw_cos - imag * tw_sin, imag * tw_cos + real * tw_sin])
        return mul("pkn,pkbw->nbw", last, turned).reshape(length, wide)

    pair = jnp.concatenate([split(k_gate * values), split(grad_out * q_gate)], axis=2)
    pair = exchange(pair).reshape(length, 2 * chans)
    filt = split(filter_raw * scale).reshape(shards, -1, FINE)
    filt = exchange(filt).reshape(length, own)

    spec = forward(pair)
    gr, gi = spec[0, :, :, :chans], spec[1, :, :, :chans]
    qr, qi = spec[0, :, :, chans:], spec[1, :, :, chans:]
    fspec = jnp.tile(forward(filt), (1, 1, 1, repeats))
    fr, fi = fspec[0], fspec[1]
    conv = jnp.stack([fr * gr - fi * gi, fr * gi + fi * gr])
    adj = jnp.stack([fr * qr + fi * qi, fr * qi - fi * qr])
    corr = jnp.stack([gr * qr + gi * qi, gr * qi - gi * qr])
    corr = corr.reshape(2, n1, FINE, repeats, own).sum(axis=3)
    out = inverse(jnp.concatenate([conv, adj], axis=3)).reshape(shards, rows, 2 * chans)
    lags = inverse(corr).reshape(shards, -1, FINE)
    out = exchange(out)
    lags = exchange(lax.psum(lags, "chan") * scale).reshape(shards, rows, own)

    grad_gated = merge(out[:, :, chans:])
    return (
        grad_out * merge(out[:, :, :chans]),
        grad_gated * values,
        grad_gated * k_gate,
        merge(lags),
    )


def solution(mesh):
    placed = P("seq", "chan")
    return jax.shard_map(
        local,
        mesh=mesh,
        in_specs=(placed, placed, placed, P("seq", None), placed),
        out_specs=(placed, placed, placed, P("seq", None)),
        check_vma=False,
    )
```

```python
import jax
import jax.numpy as jnp
import numpy as np
from jax import lax
from jax.experimental import pallas as pl
from jax.experimental.pallas import tpu as pltpu
from jax.sharding import PartitionSpec as P

FINE = 128


def mul(form, left, right):
    return jnp.einsum(form, left, right, precision=lax.Precision.HIGH)


def tables(length):
    n1 = length // FINE
    k = np.arange(n1) + 0.25
    coarse = 2.0 * np.pi * np.outer(k, np.arange(n1)) / n1
    first = np.stack([np.cos(coarse), -np.sin(coarse)])
    last = np.stack([np.cos(coarse), -np.sin(coarse)]) / length
    twist = 2.0 * np.pi * np.outer(k, np.arange(FINE)) / length
    fine = 2.0 * np.pi * (np.outer(np.arange(FINE), np.arange(FINE)) % FINE) / FINE
    cos, sin = np.cos(fine), np.sin(fine)
    ahead = np.stack([np.stack([cos, sin]), np.stack([-sin, cos])])
    back = np.stack([np.stack([cos, -sin]), np.stack([sin, cos])])
    return [np.asarray(t, np.float32) for t in (first, last, np.cos(twist), np.sin(twist), ahead, back)]


def halves(table):
    high = table.astype(jnp.bfloat16)
    return high, (table - high.astype(np.float32)).astype(jnp.bfloat16)


def split_value(x):
    high = x.astype(jnp.bfloat16)
    return high, (x - high.astype(jnp.float32)).astype(jnp.bfloat16)


def dot(left, right):
    return jnp.dot(left, right, preferred_element_type=jnp.float32)


def kernel_tables(length):
    n1 = length // FINE
    k = np.arange(n1) + 0.25
    pos = np.arange(n1)[None, :] * FINE + np.arange(FINE)[:, None]
    angle = 2.0 * np.pi * (k[None, :, None] * pos[:, None, :]) / length
    ahead = np.concatenate([np.cos(angle), -np.sin(angle)], axis=1).astype(np.float32)
    back = np.swapaxes(ahead, 1, 2) / np.float32(length)
    ah, al = halves(ahead)
    bh, bl = halves(back)
    first = np.concatenate([ah, al, ah], axis=2)
    last = np.concatenate([bh, bl, bh], axis=2)
    fine = 2.0 * np.pi * (np.outer(np.arange(FINE), np.arange(FINE)) % FINE) / FINE
    cos, sin = np.cos(fine), np.sin(fine)
    fwd = np.block([[cos, sin], [-sin, cos]]).astype(np.float32)
    inv = np.block([[cos, -sin], [sin, cos]]).astype(np.float32)
    return first, last, np.stack([np.concatenate(halves(m)) for m in (fwd, inv)])


def fold_tables(own, chans):
    spots = FINE // own
    lane = np.arange(FINE)
    spread = np.zeros((spots, FINE, FINE), np.float32)
    fold = np.zeros((spots, FINE, FINE), np.float32)
    for j in range(spots):
        spread[j, own * j + lane % own, lane] = 1.0
        used = lane[:chans]
        fold[j, used, own * j + used % own] = 1.0
    return spread.astype(jnp.bfloat16), fold.astype(jnp.bfloat16)


def order_table(width, nfilt, own):
    repeats, shards = width // nfilt, nfilt // own
    cols = np.arange(width).reshape(repeats, shards, own).transpose(1, 0, 2).reshape(-1)
    table = np.zeros((width, width), np.float32)
    table[cols, np.arange(width)] = 1.0
    return table.astype(jnp.bfloat16)


def low_lanes(rows):
    return lax.broadcasted_iota(jnp.int32, (rows, FINE), 1) < FINE // 2


def pack_kernel(k_ref, v_ref, o_ref, q_ref, table_ref, out_ref):
    table = table_ref[...]
    low = low_lanes(k_ref.shape[0])
    moved = []
    for block in (k_ref[...] * v_ref[...], o_ref[...] * q_ref[...]):
        high, rest = split_value(block)
        moved.append(dot(high, table) + dot(rest, table))
    for j in range(out_ref.shape[0] // 2):
        g, q = (m[:, FINE * j : FINE * (j + 1)] for m in moved)
        out_ref[2 * j] = jnp.where(low, g, pltpu.roll(q, FINE // 2, 1))
        out_ref[2 * j + 1] = jnp.where(low, pltpu.roll(g, FINE // 2, 1), q)


def unpack_kernel(in_ref, k_ref, v_ref, o_ref, table_ref, gq_ref, gk_ref, gv_ref):
    table = table_ref[...]
    low = low_lanes(k_ref.shape[0])
    conv, adj = [], []
    for j in range(in_ref.shape[0] // 2):
        a, b = in_ref[2 * j], in_ref[2 * j + 1]
        conv.append(jnp.where(low, a, pltpu.roll(b, FINE // 2, 1)))
        adj.append(jnp.where(low, pltpu.roll(a, FINE // 2, 1), b))
    moved = []
    for parts in (conv, adj):
        high, rest = split_value(jnp.concatenate(parts, axis=1))
        moved.append(dot(high, table) + dot(rest, table))
    gq_ref[...] = o_ref[...] * moved[0]
    gk_ref[...] = moved[1] * v_ref[...]
    gv_ref[...] = moved[1] * k_ref[...]


STEPS = 8
PITCH = FINE + 8


def fine(fine_ref, which, re, im):
    high, rest = split_value(jnp.concatenate([re, im], axis=0))
    both = dot(fine_ref[which], high)
    return both[: 2 * FINE] + (both[2 * FINE :] + dot(fine_ref[which, : 2 * FINE, :], rest))


def coarse(step, table_ref, src_ref, lines_in, dst_ref, lines_out):
    count = table_ref.shape[0]
    for j in range(count):
        n2 = step * count + j
        high, rest = split_value(src_ref[pl.ds(n2, lines_in, stride=PITCH), :])
        dst_ref[pl.ds(n2, lines_out, stride=PITCH), :] = dot(
            table_ref[j], jnp.concatenate([high, high, rest], axis=0)
        )


def side_by_side(spec_ref, at):
    return jnp.concatenate([spec_ref[a, :] for a in at], axis=1)


def lines(spec_ref, n1, k1):
    at = [pl.multiple_of(p * PITCH, 8) for p in (k1, k1 + n1)]
    return [pl.ds(p, FINE) for p in at]


def filter_kernel(filt_ref, first_ref, fine_ref, spread_ref, out_ref, wide_ref, space_ref, spec_ref):
    i = pl.program_id(0)
    n1 = space_ref.shape[0] // PITCH
    spots = spread_ref.shape[0]
    group = out_ref.shape[1]

    @pl.when(i == 0)
    def _():
        high, rest = split_value(filt_ref[...])
        short = filt_ref.shape[0]
        for j in range(spots):
            e = spread_ref[j]
            wide_ref[pl.ds(j, short, stride=spots), :] = dot(high, e) + dot(rest, e)
        for line in range(n1):
            space_ref[line * PITCH : line * PITCH + FINE, :] = wide_ref[line * FINE : (line + 1) * FINE, :]

    @pl.when(i < STEPS)
    def _():
        coarse(i, first_ref, space_ref, n1, spec_ref, 2 * n1)

    @pl.when(i >= STEPS)
    def _():
        for j in range(0, group, 2):
            at_re, at_im = zip(*(lines(spec_ref, n1, (i - STEPS) * group + j + e) for e in (0, 1)))
            z = fine(fine_ref, 0, side_by_side(spec_ref, at_re), side_by_side(spec_ref, at_im))
            for e in (0, 1):
                out_ref[0, j + e] = z[:FINE, e * FINE : (e + 1) * FINE]
                out_ref[1, j + e] = z[FINE:, e * FINE : (e + 1) * FINE]


def main_kernel(pair_ref, fspec_ref, first_ref, last_ref, fine_ref, out_ref, corr_ref, space_ref, spec_ref):
    i = pl.program_id(0)
    n1 = space_ref.shape[0] // PITCH
    group = fspec_ref.shape[1]

    @pl.when(i == 0)
    def _():
        for line in range(n1):
            space_ref[line * PITCH : line * PITCH + FINE, :] = pair_ref[line * FINE : (line + 1) * FINE, :]

    @pl.when(i < STEPS)
    def _():
        coarse(i, first_ref, space_ref, n1, spec_ref, 2 * n1)

    @pl.when((i >= STEPS) & (i < 2 * STEPS))
    def _():
        sign = jnp.where(low_lanes(FINE), 1.0, -1.0)
        for j in range(0, group, 2):
            at_re, at_im = zip(*(lines(spec_ref, n1, (i - STEPS) * group + j + e) for e in (0, 1)))
            z = fine(fine_ref, 0, side_by_side(spec_ref, at_re), side_by_side(spec_ref, at_im))
            prod = []
            for e in (0, 1):
                pr, pi = (z[p * FINE : (p + 1) * FINE, e * FINE : (e + 1) * FINE] for p in (0, 1))
                fr, fi = fspec_ref[0, j + e], fspec_ref[1, j + e] * sign
                qr, qi = pltpu.roll(pr, FINE // 2, 1), pltpu.roll(pi, FINE // 2, 1)
                corr_ref[0, j + e] = pr * qr + pi * qi
                corr_ref[1, j + e] = pr * qi - pi * qr
                prod.append((fr * pr - fi * pi, fr * pi + fi * pr))
            w = fine(fine_ref, 1, *(jnp.concatenate(part, axis=1) for part in zip(*prod)))
            for e in (0, 1):
                spec_ref[at_re[e], :] = w[:FINE, e * FINE : (e + 1) * FINE]
                spec_ref[at_im[e], :] = w[FINE:, e * FINE : (e + 1) * FINE]

    @pl.when(i >= 2 * STEPS)
    def _():
        coarse(i - 2 * STEPS, last_ref, spec_ref, 2 * n1, space_ref, n1)

    @pl.when(i == 3 * STEPS - 1)
    def _():
        for line in range(n1):
            out_ref[line * FINE : (line + 1) * FINE, :] = space_ref[line * PITCH : line * PITCH + FINE, :]


def lags_kernel(corr_ref, last_ref, fine_ref, fold_ref, lags_ref, wide_ref, space_ref, spec_ref):
    i = pl.program_id(0)
    n1 = space_ref.shape[0] // PITCH
    spots = fold_ref.shape[0]
    group = corr_ref.shape[1]

    @pl.when(i < STEPS)
    def _():
        for j in range(0, group, 2):
            at_re, at_im = zip(*(lines(spec_ref, n1, i * group + j + e) for e in (0, 1)))
            w = fine(
                fine_ref, 1, *(jnp.concatenate([corr_ref[p, j], corr_ref[p, j + 1]], axis=1) for p in (0, 1))
            )
            for e in (0, 1):
                spec_ref[at_re[e], :] = w[:FINE, e * FINE : (e + 1) * FINE]
                spec_ref[at_im[e], :] = w[FINE:, e * FINE : (e + 1) * FINE]

    @pl.when(i >= STEPS)
    def _():
        coarse(i - STEPS, last_ref, spec_ref, 2 * n1, space_ref, n1)

    @pl.when(i == 2 * STEPS - 1)
    def _():
        for line in range(n1):
            wide_ref[line * FINE : (line + 1) * FINE, :] = space_ref[line * PITCH : line * PITCH + FINE, :]
        short = lags_ref.shape[0]
        total = jnp.zeros((short, FINE), jnp.float32)
        for j in range(spots):
            high, rest = split_value(wide_ref[pl.ds(j, short, stride=spots), :])
            total += dot(high, fold_ref[j]) + dot(rest, fold_ref[j])
        lags_ref[...] = total


VMEM_BYTES = 60 << 20


def pack(k_gate, values, grad_out, q_gate, shards, table):
    rows, width = k_gate.shape
    tile = 128
    block = pl.BlockSpec((tile, width), lambda i: (i, 0))
    return pl.pallas_call(
        pack_kernel,
        grid=(rows // tile,),
        in_specs=[block] * 4 + [pl.BlockSpec((width, width), lambda i: (0, 0))],
        out_specs=pl.BlockSpec((shards, tile, FINE), lambda i: (0, i, 0)),
        out_shape=jax.ShapeDtypeStruct((shards, rows, FINE), jnp.float32),
        compiler_params=pltpu.CompilerParams(vmem_limit_bytes=VMEM_BYTES),
        cost_estimate=pl.CostEstimate(
            flops=8 * rows * width * width, bytes_accessed=24 * rows * width, transcendentals=0
        ),
        name="pack",
    )(k_gate, values, grad_out, q_gate, table)


def unpack(back, k_gate, values, grad_out, table):
    rows, width = k_gate.shape
    tile = 128
    block = pl.BlockSpec((tile, width), lambda i: (i, 0))
    return pl.pallas_call(
        unpack_kernel,
        grid=(rows // tile,),
        in_specs=[pl.BlockSpec((back.shape[0], tile, FINE), lambda i: (0, i, 0))]
        + [block] * 3
        + [pl.BlockSpec((width, width), lambda i: (0, 0))],
        out_specs=[block] * 3,
        out_shape=[jax.ShapeDtypeStruct((rows, width), jnp.float32)] * 3,
        compiler_params=pltpu.CompilerParams(vmem_limit_bytes=VMEM_BYTES),
        cost_estimate=pl.CostEstimate(
            flops=8 * rows * width * width, bytes_accessed=32 * rows * width, transcendentals=0
        ),
        name="unpack",
    )(back, k_gate, values, grad_out, table)


def whole(array):
    return pl.BlockSpec(array.shape, lambda i: (0,) * len(array.shape))


def phase(array, axis, start):
    block = tuple(d // STEPS if a == axis else d for a, d in enumerate(array.shape))

    def index(i):
        at = jnp.clip(i - start, 0, STEPS - 1)
        return tuple(at if a == axis else 0 for a in range(len(block)))

    return pl.BlockSpec(block, index)


def stepped(kernel, phases, ins, in_specs, outs, out_specs, scratch, flops, name):
    return pl.pallas_call(
        kernel,
        grid=(phases * STEPS,),
        in_specs=in_specs,
        out_specs=out_specs,
        out_shape=outs,
        scratch_shapes=[pltpu.VMEM((rows, FINE), jnp.float32) for rows in scratch],
        compiler_params=pltpu.CompilerParams(vmem_limit_bytes=VMEM_BYTES),
        cost_estimate=pl.CostEstimate(
            flops=flops, bytes_accessed=24 << 20, transcendentals=0
        ),
        name=name,
    )(*ins)


def spectral(length, own, chans):
    n1 = length // FINE
    first, last, mats = (jnp.asarray(t) for t in kernel_tables(length))
    spread, fold = (jnp.asarray(t) for t in fold_tables(own, chans))
    spec = jax.ShapeDtypeStruct((2, n1, FINE, FINE), jnp.float32)
    space = jax.ShapeDtypeStruct((length, FINE), jnp.float32)
    packed = jax.ShapeDtypeStruct((length * own // FINE, FINE), jnp.float32)
    padded = [n1 * PITCH, 2 * n1 * PITCH]

    def filter_stage(filt):
        return stepped(
            filter_kernel, 2, (filt, first, mats, spread),
            [whole(filt), phase(first, 0, 0), whole(mats), whole(spread)],
            spec, phase(spec, 1, STEPS), [length] + padded, 15_000_000_000, "filter_spectrum",
        )

    def main_stage(pair, fspec):
        return stepped(
            main_kernel, 3, (pair, fspec, first, last, mats),
            [whole(pair), phase(fspec, 1, STEPS), phase(first, 0, 0), phase(last, 0, 2 * STEPS), whole(mats)],
            [space, spec], [whole(space), phase(spec, 1, STEPS)], padded, 30_000_000_000, "pair_stage",
        )

    def lags_stage(corr):
        return stepped(
            lags_kernel, 2, (corr, last, mats, fold),
            [phase(corr, 1, 0), phase(last, 0, STEPS), whole(mats), whole(fold)],
            packed, whole(packed), [length] + padded, 15_000_000_000, "lags",
        )

    return filter_stage, main_stage, lags_stage


def local(q_gate, k_gate, values, filter_raw, grad_out):
    rows, width = q_gate.shape
    nfilt = filter_raw.shape[1]
    shards = lax.axis_size("seq")
    length = rows * shards
    repeats = width // nfilt
    own = nfilt // shards
    chans = repeats * own
    scale = float(length) ** (-0.5)
    n1 = length // FINE
    first, last, tw_cos, tw_sin, ahead, back = tables(length)
    tw_cos = tw_cos[None, :, :, None][0]
    tw_sin = tw_sin[None, :, :, None][0]

    def split(block):
        groups = block.shape[1] // nfilt
        parts = block.reshape(rows, groups, shards, own)
        return parts.transpose(2, 0, 1, 3).reshape(shards, rows, groups * own)

    def merge(parts):
        groups = parts.shape[2] // own
        block = parts.reshape(shards, rows, groups, own).transpose(1, 2, 0, 3)
        return block.reshape(rows, groups * nfilt)

    def exchange(parts):
        return lax.all_to_all(parts, "seq", split_axis=0, concat_axis=0, tiled=True)

    if 2 * chans == FINE and n1 == 64:
        table = order_table(width, nfilt, own)
        filt = exchange(split(filter_raw * scale).reshape(shards, -1, FINE))
        pair = exchange(pack(k_gate, values, grad_out, q_gate, shards, jnp.asarray(table)))
        filter_stage, main_stage, lags_stage = spectral(length, own, chans)
        fspec = filter_stage(filt.reshape(-1, FINE))
        out, corr = main_stage(pair.reshape(length, FINE), fspec)
        out = exchange(out.reshape(shards, rows, FINE))
        lags = lax.psum(lags_stage(corr), "chan") * scale
        lags, _ = lax.optimization_barrier((lags, out))
        lags = merge(exchange(lags.reshape(shards, -1, FINE)).reshape(shards, rows, own))
        return tuple(unpack(out, k_gate, values, grad_out, jnp.asarray(table.T))) + (lags,)

    def forward(block):
        wide = block.shape[1]
        part = mul("pkn,nbw->pkbw", first, block.reshape(n1, FINE, wide))
        real, imag = part[0], part[1]
        turned = jnp.stack([real * tw_cos + imag * tw_sin, imag * tw_cos - real * tw_sin])
        return mul("opkn,ptnw->otkw", ahead, turned)

    def inverse(spec):
        wide = spec.shape[3]
        part = mul("opkn,ptnw->otkw", back, spec)
        real, imag = part[0], part[1]
        turned = jnp.stack([real * tw_cos - imag * tw_sin, imag * tw_cos + real * tw_sin])
        return mul("pkn,pkbw->nbw", last, turned).reshape(length, wide)

    pair = jnp.concatenate([split(k_gate * values), split(grad_out * q_gate)], axis=2)
    pair = exchange(pair).reshape(length, 2 * chans)
    filt = split(filter_raw * scale).reshape(shards, -1, FINE)
    filt = exchange(filt).reshape(length, own)

    spec = forward(pair)
    gr, gi = spec[0, :, :, :chans], spec[1, :, :, :chans]
    qr, qi = spec[0, :, :, chans:], spec[1, :, :, chans:]
    fspec = jnp.tile(forward(filt), (1, 1, 1, repeats))
    fr, fi = fspec[0], fspec[1]
    conv = jnp.stack([fr * gr - fi * gi, fr * gi + fi * gr])
    adj = jnp.stack([fr * qr + fi * qi, fr * qi - fi * qr])
    corr = jnp.stack([gr * qr + gi * qi, gr * qi - gi * qr])
    corr = corr.reshape(2, n1, FINE, repeats, own).sum(axis=3)
    out = inverse(jnp.concatenate([conv, adj], axis=3)).reshape(shards, rows, 2 * chans)
    lags = inverse(corr).reshape(shards, -1, FINE)
    out = exchange(out)
    lags = exchange(lax.psum(lags, "chan") * scale).reshape(shards, rows, own)

    grad_gated = merge(out[:, :, chans:])
    return (
        grad_out * merge(out[:, :, :chans]),
        grad_gated * values,
        grad_gated * k_gate,
        merge(lags),
    )


def solution(mesh):
    placed = P("seq", "chan")
    return jax.shard_map(
        local,
        mesh=mesh,
        in_specs=(placed, placed, placed, P("seq", None), placed),
        out_specs=(placed, placed, placed, P("seq", None)),
        check_vma=False,
    )
```

```python
import functools

import jax
import jax.numpy as jnp
import numpy as np
from jax import lax
from jax.experimental import pallas as pl
from jax.experimental.pallas import tpu as pltpu
from jax.sharding import PartitionSpec as P

FINE = 128


def mul(form, left, right):
    return jnp.einsum(form, left, right, precision=lax.Precision.HIGH)


def tables(length):
    n1 = length // FINE
    k = np.arange(n1) + 0.25
    coarse = 2.0 * np.pi * np.outer(k, np.arange(n1)) / n1
    first = np.stack([np.cos(coarse), -np.sin(coarse)])
    last = np.stack([np.cos(coarse), -np.sin(coarse)]) / length
    twist = 2.0 * np.pi * np.outer(k, np.arange(FINE)) / length
    fine = 2.0 * np.pi * (np.outer(np.arange(FINE), np.arange(FINE)) % FINE) / FINE
    cos, sin = np.cos(fine), np.sin(fine)
    ahead = np.stack([np.stack([cos, sin]), np.stack([-sin, cos])])
    back = np.stack([np.stack([cos, -sin]), np.stack([sin, cos])])
    return [np.asarray(t, np.float32) for t in (first, last, np.cos(twist), np.sin(twist), ahead, back)]


def halves(table):
    high = table.astype(jnp.bfloat16)
    return high, (table - high.astype(np.float32)).astype(jnp.bfloat16)


def split_value(x):
    high = x.astype(jnp.bfloat16)
    return high, (x - high.astype(jnp.float32)).astype(jnp.bfloat16)


def dot(left, right):
    return jnp.dot(left, right, preferred_element_type=jnp.float32)


def kernel_tables(length):
    n1 = length // FINE
    k = np.arange(n1) + 0.25
    pos = np.arange(n1)[None, :] * FINE + np.arange(FINE)[:, None]
    angle = 2.0 * np.pi * (k[None, :, None] * pos[:, None, :]) / length
    ahead = np.concatenate([np.cos(angle), -np.sin(angle)], axis=1).astype(np.float32)
    back = np.swapaxes(ahead, 1, 2) / np.float32(length)
    ah, al = halves(ahead)
    bh, bl = halves(back)
    first = np.concatenate([ah, al, ah], axis=2)
    last = np.concatenate([bh, bl, bh], axis=2)
    fine = 2.0 * np.pi * (np.outer(np.arange(FINE), np.arange(FINE)) % FINE) / FINE
    cos, sin = np.cos(fine), np.sin(fine)
    fwd = np.block([[cos, sin], [-sin, cos]]).astype(np.float32)
    inv = np.block([[cos, -sin], [sin, cos]]).astype(np.float32)
    return first, last, np.stack([np.concatenate(halves(m)) for m in (fwd, inv)])


def fold_tables(own, chans):
    spots = FINE // own
    lane = np.arange(FINE)
    spread = np.zeros((spots, FINE, FINE), np.float32)
    fold = np.zeros((spots, FINE, FINE), np.float32)
    for j in range(spots):
        spread[j, own * j + lane % own, lane] = 1.0
        used = lane[:chans]
        fold[j, used, own * j + used % own] = 1.0
    return spread.astype(jnp.bfloat16), fold.astype(jnp.bfloat16)


def order_table(width, nfilt, own):
    repeats, shards = width // nfilt, nfilt // own
    cols = np.arange(width).reshape(repeats, shards, own).transpose(1, 0, 2).reshape(-1)
    table = np.zeros((width, width), np.float32)
    table[cols, np.arange(width)] = 1.0
    return table.astype(jnp.bfloat16)


def low_lanes(rows):
    return lax.broadcasted_iota(jnp.int32, (rows, FINE), 1) < FINE // 2


def pack_kernel(k_ref, v_ref, o_ref, q_ref, table_ref, out_ref):
    table = table_ref[...]
    low = low_lanes(k_ref.shape[0])
    moved = []
    for block in (k_ref[...] * v_ref[...], o_ref[...] * q_ref[...]):
        high, rest = split_value(block)
        moved.append(dot(high, table) + dot(rest, table))
    for j in range(out_ref.shape[0] // 2):
        g, q = (m[:, FINE * j : FINE * (j + 1)] for m in moved)
        out_ref[2 * j] = jnp.where(low, g, pltpu.roll(q, FINE // 2, 1))
        out_ref[2 * j + 1] = jnp.where(low, pltpu.roll(g, FINE // 2, 1), q)


def unpack_kernel(in_ref, k_ref, v_ref, o_ref, table_ref, gq_ref, gk_ref, gv_ref):
    table = table_ref[...]
    low = low_lanes(k_ref.shape[0])
    conv, adj = [], []
    for j in range(in_ref.shape[0] // 2):
        a, b = in_ref[2 * j], in_ref[2 * j + 1]
        conv.append(jnp.where(low, a, pltpu.roll(b, FINE // 2, 1)))
        adj.append(jnp.where(low, pltpu.roll(a, FINE // 2, 1), b))
    moved = []
    for parts in (conv, adj):
        high, rest = split_value(jnp.concatenate(parts, axis=1))
        moved.append(dot(high, table) + dot(rest, table))
    gq_ref[...] = o_ref[...] * moved[0]
    gk_ref[...] = moved[1] * v_ref[...]
    gv_ref[...] = moved[1] * k_ref[...]


STEPS = 8
PITCH = FINE + 8


def fine(fine_ref, which, re, im):
    high, rest = split_value(jnp.concatenate([re, im], axis=0))
    both = dot(fine_ref[which], high)
    return both[: 2 * FINE] + (both[2 * FINE :] + dot(fine_ref[which, : 2 * FINE, :], rest))


def coarse(step, table_ref, src_ref, lines_in, dst_ref, lines_out):
    count = table_ref.shape[0]
    for j in range(count):
        n2 = step * count + j
        high, rest = split_value(src_ref[pl.ds(n2, lines_in, stride=PITCH), :])
        dst_ref[pl.ds(n2, lines_out, stride=PITCH), :] = dot(
            table_ref[j], jnp.concatenate([high, high, rest], axis=0)
        )


def side_by_side(spec_ref, at):
    return jnp.concatenate([spec_ref[a, :] for a in at], axis=1)


def lines(spec_ref, n1, k1):
    at = [pl.multiple_of(p * PITCH, 8) for p in (k1, k1 + n1)]
    return [pl.ds(p, FINE) for p in at]


def filter_kernel(scale, filt_ref, first_ref, fine_ref, spread_ref, out_ref, wide_ref, space_ref, spec_ref):
    i = pl.program_id(0)
    n1 = space_ref.shape[0] // PITCH
    spots = spread_ref.shape[0]
    group = out_ref.shape[1]

    @pl.when(i == 0)
    def _():
        high, rest = split_value(filt_ref[...])
        short = filt_ref.shape[0]
        for j in range(spots):
            e = spread_ref[j]
            wide_ref[pl.ds(j, short, stride=spots), :] = scale * (dot(high, e) + dot(rest, e))
        for line in range(n1):
            space_ref[line * PITCH : line * PITCH + FINE, :] = wide_ref[line * FINE : (line + 1) * FINE, :]

    @pl.when(i < STEPS)
    def _():
        coarse(i, first_ref, space_ref, n1, spec_ref, 2 * n1)

    @pl.when(i >= STEPS)
    def _():
        for j in range(0, group, 2):
            at_re, at_im = zip(*(lines(spec_ref, n1, (i - STEPS) * group + j + e) for e in (0, 1)))
            z = fine(fine_ref, 0, side_by_side(spec_ref, at_re), side_by_side(spec_ref, at_im))
            for e in (0, 1):
                out_ref[0, j + e] = z[:FINE, e * FINE : (e + 1) * FINE]
                out_ref[1, j + e] = z[FINE:, e * FINE : (e + 1) * FINE]


def main_kernel(pair_ref, fspec_ref, first_ref, last_ref, fine_ref, out_ref, corr_ref, space_ref, spec_ref):
    i = pl.program_id(0)
    n1 = space_ref.shape[0] // PITCH
    group = fspec_ref.shape[1]

    @pl.when(i == 0)
    def _():
        for line in range(n1):
            space_ref[line * PITCH : line * PITCH + FINE, :] = pair_ref[line * FINE : (line + 1) * FINE, :]

    @pl.when(i < STEPS)
    def _():
        coarse(i, first_ref, space_ref, n1, spec_ref, 2 * n1)

    @pl.when((i >= STEPS) & (i < 2 * STEPS))
    def _():
        sign = jnp.where(low_lanes(FINE), 1.0, -1.0)
        for j in range(0, group, 2):
            at_re, at_im = zip(*(lines(spec_ref, n1, (i - STEPS) * group + j + e) for e in (0, 1)))
            z = fine(fine_ref, 0, side_by_side(spec_ref, at_re), side_by_side(spec_ref, at_im))
            prod = []
            for e in (0, 1):
                pr, pi = (z[p * FINE : (p + 1) * FINE, e * FINE : (e + 1) * FINE] for p in (0, 1))
                fr, fi = fspec_ref[0, j + e], fspec_ref[1, j + e] * sign
                qr, qi = pltpu.roll(pr, FINE // 2, 1), pltpu.roll(pi, FINE // 2, 1)
                corr_ref[0, j + e] = pr * qr + pi * qi
                corr_ref[1, j + e] = pr * qi - pi * qr
                prod.append((fr * pr - fi * pi, fr * pi + fi * pr))
            w = fine(fine_ref, 1, *(jnp.concatenate(part, axis=1) for part in zip(*prod)))
            for e in (0, 1):
                spec_ref[at_re[e], :] = w[:FINE, e * FINE : (e + 1) * FINE]
                spec_ref[at_im[e], :] = w[FINE:, e * FINE : (e + 1) * FINE]

    @pl.when(i >= 2 * STEPS)
    def _():
        coarse(i - 2 * STEPS, last_ref, spec_ref, 2 * n1, space_ref, n1)

    @pl.when(i == 3 * STEPS - 1)
    def _():
        for line in range(n1):
            out_ref[line * FINE : (line + 1) * FINE, :] = space_ref[line * PITCH : line * PITCH + FINE, :]


def lags_kernel(corr_ref, last_ref, fine_ref, fold_ref, lags_ref, wide_ref, space_ref, spec_ref):
    i = pl.program_id(0)
    n1 = space_ref.shape[0] // PITCH
    spots = fold_ref.shape[0]
    group = corr_ref.shape[1]

    @pl.when(i < STEPS)
    def _():
        for j in range(0, group, 2):
            at_re, at_im = zip(*(lines(spec_ref, n1, i * group + j + e) for e in (0, 1)))
            w = fine(
                fine_ref, 1, *(jnp.concatenate([corr_ref[p, j], corr_ref[p, j + 1]], axis=1) for p in (0, 1))
            )
            for e in (0, 1):
                spec_ref[at_re[e], :] = w[:FINE, e * FINE : (e + 1) * FINE]
                spec_ref[at_im[e], :] = w[FINE:, e * FINE : (e + 1) * FINE]

    @pl.when(i >= STEPS)
    def _():
        coarse(i - STEPS, last_ref, spec_ref, 2 * n1, space_ref, n1)

    @pl.when(i == 2 * STEPS - 1)
    def _():
        for line in range(n1):
            wide_ref[line * FINE : (line + 1) * FINE, :] = space_ref[line * PITCH : line * PITCH + FINE, :]
        short = lags_ref.shape[0]
        total = jnp.zeros((short, FINE), jnp.float32)
        for j in range(spots):
            high, rest = split_value(wide_ref[pl.ds(j, short, stride=spots), :])
            total += dot(high, fold_ref[j]) + dot(rest, fold_ref[j])
        lags_ref[...] = total


VMEM_BYTES = 60 << 20


def pack(k_gate, values, grad_out, q_gate, shards, table):
    rows, width = k_gate.shape
    tile = 128
    block = pl.BlockSpec((tile, width), lambda i: (i, 0))
    return pl.pallas_call(
        pack_kernel,
        grid=(rows // tile,),
        in_specs=[block] * 4 + [pl.BlockSpec((width, width), lambda i: (0, 0))],
        out_specs=pl.BlockSpec((shards, tile, FINE), lambda i: (0, i, 0)),
        out_shape=jax.ShapeDtypeStruct((shards, rows, FINE), jnp.float32),
        compiler_params=pltpu.CompilerParams(vmem_limit_bytes=VMEM_BYTES),
        cost_estimate=pl.CostEstimate(
            flops=8 * rows * width * width, bytes_accessed=24 * rows * width, transcendentals=0
        ),
        name="pack",
    )(k_gate, values, grad_out, q_gate, table)


def unpack(back, k_gate, values, grad_out, table):
    rows, width = k_gate.shape
    tile = 128
    block = pl.BlockSpec((tile, width), lambda i: (i, 0))
    return pl.pallas_call(
        unpack_kernel,
        grid=(rows // tile,),
        in_specs=[pl.BlockSpec((back.shape[0], tile, FINE), lambda i: (0, i, 0))]
        + [block] * 3
        + [pl.BlockSpec((width, width), lambda i: (0, 0))],
        out_specs=[block] * 3,
        out_shape=[jax.ShapeDtypeStruct((rows, width), jnp.float32)] * 3,
        compiler_params=pltpu.CompilerParams(vmem_limit_bytes=VMEM_BYTES),
        cost_estimate=pl.CostEstimate(
            flops=8 * rows * width * width, bytes_accessed=32 * rows * width, transcendentals=0
        ),
        name="unpack",
    )(back, k_gate, values, grad_out, table)


def whole(array):
    return pl.BlockSpec(array.shape, lambda i: (0,) * len(array.shape))


def phase(array, axis, start):
    block = tuple(d // STEPS if a == axis else d for a, d in enumerate(array.shape))

    def index(i):
        at = jnp.clip(i - start, 0, STEPS - 1)
        return tuple(at if a == axis else 0 for a in range(len(block)))

    return pl.BlockSpec(block, index)


def stepped(kernel, phases, ins, in_specs, outs, out_specs, scratch, flops, name):
    return pl.pallas_call(
        kernel,
        grid=(phases * STEPS,),
        in_specs=in_specs,
        out_specs=out_specs,
        out_shape=outs,
        scratch_shapes=[pltpu.VMEM((rows, FINE), jnp.float32) for rows in scratch],
        compiler_params=pltpu.CompilerParams(vmem_limit_bytes=VMEM_BYTES),
        cost_estimate=pl.CostEstimate(
            flops=flops, bytes_accessed=24 << 20, transcendentals=0
        ),
        name=name,
    )(*ins)


def spectral(length, own, chans):
    n1 = length // FINE
    first, last, mats = (jnp.asarray(t) for t in kernel_tables(length))
    spread, fold = (jnp.asarray(t) for t in fold_tables(own, chans))
    spec = jax.ShapeDtypeStruct((2, n1, FINE, FINE), jnp.float32)
    space = jax.ShapeDtypeStruct((length, FINE), jnp.float32)
    packed = jax.ShapeDtypeStruct((length * own // FINE, FINE), jnp.float32)
    padded = [n1 * PITCH, 2 * n1 * PITCH]

    def filter_stage(filt):
        return stepped(
            functools.partial(filter_kernel, float(length) ** -0.5), 2, (filt, first, mats, spread),
            [whole(filt), phase(first, 0, 0), whole(mats), whole(spread)],
            spec, phase(spec, 1, STEPS), [length] + padded, 15_000_000_000, "filter_spectrum",
        )

    def main_stage(pair, fspec):
        return stepped(
            main_kernel, 3, (pair, fspec, first, last, mats),
            [whole(pair), phase(fspec, 1, STEPS), phase(first, 0, 0), phase(last, 0, 2 * STEPS), whole(mats)],
            [space, spec], [whole(space), phase(spec, 1, STEPS)], padded, 30_000_000_000, "pair_stage",
        )

    def lags_stage(corr):
        return stepped(
            lags_kernel, 2, (corr, last, mats, fold),
            [phase(corr, 1, 0), phase(last, 0, STEPS), whole(mats), whole(fold)],
            packed, whole(packed), [length] + padded, 15_000_000_000, "lags",
        )

    return filter_stage, main_stage, lags_stage


def place_kernel(*refs):
    me = lax.axis_index("seq")
    out_ref = refs[-1]
    shards = out_ref.shape[0]
    for hop in range(shards):
        out_ref[lax.rem(me + shards - hop, shards)] = refs[hop][0]


def scatter_around(parts, shards):
    me = lax.axis_index("seq")
    came = []
    for hop in range(shards):
        part = lax.dynamic_index_in_dim(parts, (me + hop) % shards, 0, keepdims=True)
        if hop:
            part = lax.ppermute(part, "seq", [(i, (i + hop) % shards) for i in range(shards)])
        came.append(part)
    vmem = pl.BlockSpec(memory_space=pltpu.VMEM)
    return pl.pallas_call(
        place_kernel,
        in_specs=[vmem] * shards,
        out_specs=vmem,
        out_shape=jax.ShapeDtypeStruct(parts.shape, parts.dtype),
        name="place",
    )(*came)


def local(q_gate, k_gate, values, filter_raw, grad_out):
    rows, width = q_gate.shape
    nfilt = filter_raw.shape[1]
    shards = lax.axis_size("seq")
    length = rows * shards
    repeats = width // nfilt
    own = nfilt // shards
    chans = repeats * own
    scale = float(length) ** (-0.5)
    n1 = length // FINE
    first, last, tw_cos, tw_sin, ahead, back = tables(length)
    tw_cos = tw_cos[None, :, :, None][0]
    tw_sin = tw_sin[None, :, :, None][0]

    def split(block):
        groups = block.shape[1] // nfilt
        parts = block.reshape(rows, groups, shards, own)
        return parts.transpose(2, 0, 1, 3).reshape(shards, rows, groups * own)

    def merge(parts):
        groups = parts.shape[2] // own
        block = parts.reshape(shards, rows, groups, own).transpose(1, 2, 0, 3)
        return block.reshape(rows, groups * nfilt)

    def exchange(parts):
        return lax.all_to_all(parts, "seq", split_axis=0, concat_axis=0, tiled=True)

    if 2 * chans == FINE and n1 == 64:
        table = order_table(width, nfilt, own)
        filt = exchange(split(filter_raw).reshape(shards, -1, FINE))
        packed = pack(k_gate, values, grad_out, q_gate, shards, jnp.asarray(table))
        filt, packed = lax.optimization_barrier((filt, packed))
        pair = exchange(packed)
        filter_stage, main_stage, lags_stage = spectral(length, own, chans)
        fspec = filter_stage(filt.reshape(-1, FINE))
        out, corr = main_stage(pair.reshape(length, FINE), fspec)
        out = exchange(out.reshape(shards, rows, FINE))
        lags = lax.psum(lags_stage(corr), "chan") * scale
        lags = scatter_around(lags.reshape(shards, -1, FINE), shards)
        lags, _ = lax.optimization_barrier((lags, out))
        lags = merge(lags.reshape(shards, rows, own))
        return tuple(unpack(out, k_gate, values, grad_out, jnp.asarray(table.T))) + (lags,)

    def forward(block):
        wide = block.shape[1]
        part = mul("pkn,nbw->pkbw", first, block.reshape(n1, FINE, wide))
        real, imag = part[0], part[1]
        turned = jnp.stack([real * tw_cos + imag * tw_sin, imag * tw_cos - real * tw_sin])
        return mul("opkn,ptnw->otkw", ahead, turned)

    def inverse(spec):
        wide = spec.shape[3]
        part = mul("opkn,ptnw->otkw", back, spec)
        real, imag = part[0], part[1]
        turned = jnp.stack([real * tw_cos - imag * tw_sin, imag * tw_cos + real * tw_sin])
        return mul("pkn,pkbw->nbw", last, turned).reshape(length, wide)

    pair = jnp.concatenate([split(k_gate * values), split(grad_out * q_gate)], axis=2)
    pair = exchange(pair).reshape(length, 2 * chans)
    filt = split(filter_raw * scale).reshape(shards, -1, FINE)
    filt = exchange(filt).reshape(length, own)

    spec = forward(pair)
    gr, gi = spec[0, :, :, :chans], spec[1, :, :, :chans]
    qr, qi = spec[0, :, :, chans:], spec[1, :, :, chans:]
    fspec = jnp.tile(forward(filt), (1, 1, 1, repeats))
    fr, fi = fspec[0], fspec[1]
    conv = jnp.stack([fr * gr - fi * gi, fr * gi + fi * gr])
    adj = jnp.stack([fr * qr + fi * qi, fr * qi - fi * qr])
    corr = jnp.stack([gr * qr + gi * qi, gr * qi - gi * qr])
    corr = corr.reshape(2, n1, FINE, repeats, own).sum(axis=3)
    out = inverse(jnp.concatenate([conv, adj], axis=3)).reshape(shards, rows, 2 * chans)
    lags = inverse(corr).reshape(shards, -1, FINE)
    out = exchange(out)
    lags = exchange(lax.psum(lags, "chan") * scale).reshape(shards, rows, own)

    grad_gated = merge(out[:, :, chans:])
    return (
        grad_out * merge(out[:, :, :chans]),
        grad_gated * values,
        grad_gated * k_gate,
        merge(lags),
    )


def solution(mesh):
    placed = P("seq", "chan")
    return jax.shard_map(
        local,
        mesh=mesh,
        in_specs=(placed, placed, placed, P("seq", None), placed),
        out_specs=(placed, placed, placed, P("seq", None)),
        check_vma=False,
    )
```

```python
import functools

import jax
import jax.numpy as jnp
import numpy as np
from jax import lax
from jax.experimental import pallas as pl
from jax.experimental.pallas import tpu as pltpu
from jax.sharding import PartitionSpec as P

FINE = 128


def mul(form, left, right):
    return jnp.einsum(form, left, right, precision=lax.Precision.HIGH)


def tables(length):
    n1 = length // FINE
    k = np.arange(n1) + 0.25
    coarse = 2.0 * np.pi * np.outer(k, np.arange(n1)) / n1
    first = np.stack([np.cos(coarse), -np.sin(coarse)])
    last = np.stack([np.cos(coarse), -np.sin(coarse)]) / length
    twist = 2.0 * np.pi * np.outer(k, np.arange(FINE)) / length
    fine = 2.0 * np.pi * (np.outer(np.arange(FINE), np.arange(FINE)) % FINE) / FINE
    cos, sin = np.cos(fine), np.sin(fine)
    ahead = np.stack([np.stack([cos, sin]), np.stack([-sin, cos])])
    back = np.stack([np.stack([cos, -sin]), np.stack([sin, cos])])
    return [np.asarray(t, np.float32) for t in (first, last, np.cos(twist), np.sin(twist), ahead, back)]


def halves(table):
    high = table.astype(jnp.bfloat16)
    return high, (table - high.astype(np.float32)).astype(jnp.bfloat16)


def split_value(x):
    high = x.astype(jnp.bfloat16)
    return high, (x - high.astype(jnp.float32)).astype(jnp.bfloat16)


def dot(left, right):
    return jnp.dot(left, right, preferred_element_type=jnp.float32)


def kernel_tables(length):
    n1 = length // FINE
    k = np.arange(n1) + 0.25
    pos = np.arange(n1)[None, :] * FINE + np.arange(FINE)[:, None]
    angle = 2.0 * np.pi * (k[None, :, None] * pos[:, None, :]) / length
    ahead = np.concatenate([np.cos(angle), -np.sin(angle)], axis=1).astype(np.float32)
    back = np.swapaxes(ahead, 1, 2) / np.float32(length)
    ah, al = halves(ahead)
    bh, bl = halves(back)
    first = np.concatenate([ah, al, ah], axis=2)
    last = np.concatenate([bh, bl, bh], axis=2)
    fine = 2.0 * np.pi * (np.outer(np.arange(FINE), np.arange(FINE)) % FINE) / FINE
    cos, sin = np.cos(fine), np.sin(fine)
    fwd = np.block([[cos, sin], [-sin, cos]]).astype(np.float32)
    inv = np.block([[cos, -sin], [sin, cos]]).astype(np.float32)
    return first, last, np.stack([np.concatenate(halves(m)) for m in (fwd, inv)])


def fold_tables(own, chans):
    spots = FINE // own
    lane = np.arange(FINE)
    spread = np.zeros((spots, FINE, FINE), np.float32)
    fold = np.zeros((spots, FINE, FINE), np.float32)
    for j in range(spots):
        spread[j, own * j + lane % own, lane] = 1.0
        used = lane[:chans]
        fold[j, used, own * j + used % own] = 1.0
    return spread.astype(jnp.bfloat16), fold.astype(jnp.bfloat16)


def order_table(width, nfilt, own):
    repeats, shards = width // nfilt, nfilt // own
    cols = np.arange(width).reshape(repeats, shards, own).transpose(1, 0, 2).reshape(-1)
    table = np.zeros((width, width), np.float32)
    table[cols, np.arange(width)] = 1.0
    return table.astype(jnp.bfloat16)


def low_lanes(rows):
    return lax.broadcasted_iota(jnp.int32, (rows, FINE), 1) < FINE // 2


def pack_kernel(k_ref, v_ref, o_ref, q_ref, table_ref, out_ref):
    table = table_ref[...]
    low = low_lanes(k_ref.shape[0])
    moved = []
    for block in (k_ref[...] * v_ref[...], o_ref[...] * q_ref[...]):
        high, rest = split_value(block)
        moved.append(dot(high, table) + dot(rest, table))
    for j in range(out_ref.shape[0] // 2):
        g, q = (m[:, FINE * j : FINE * (j + 1)] for m in moved)
        out_ref[2 * j] = jnp.where(low, g, pltpu.roll(q, FINE // 2, 1))
        out_ref[2 * j + 1] = jnp.where(low, pltpu.roll(g, FINE // 2, 1), q)


def unpack_kernel(in_ref, k_ref, v_ref, o_ref, table_ref, gq_ref, gk_ref, gv_ref):
    table = table_ref[...]
    low = low_lanes(k_ref.shape[0])
    conv, adj = [], []
    for j in range(in_ref.shape[0] // 2):
        a, b = in_ref[2 * j], in_ref[2 * j + 1]
        conv.append(jnp.where(low, a, pltpu.roll(b, FINE // 2, 1)))
        adj.append(jnp.where(low, pltpu.roll(a, FINE // 2, 1), b))
    moved = []
    for parts in (conv, adj):
        high, rest = split_value(jnp.concatenate(parts, axis=1))
        moved.append(dot(high, table) + dot(rest, table))
    gq_ref[...] = o_ref[...] * moved[0]
    gk_ref[...] = moved[1] * v_ref[...]
    gv_ref[...] = moved[1] * k_ref[...]


STEPS = 8
PITCH = FINE + 8


def fine(fine_ref, which, re, im):
    high, rest = split_value(jnp.concatenate([re, im], axis=0))
    both = dot(fine_ref[which], high)
    return both[: 2 * FINE] + (both[2 * FINE :] + dot(fine_ref[which, : 2 * FINE, :], rest))


def coarse(step, table_ref, src_ref, lines_in, dst_ref, lines_out):
    count = table_ref.shape[0]
    for j in range(count):
        n2 = step * count + j
        high, rest = split_value(src_ref[pl.ds(n2, lines_in, stride=PITCH), :])
        dst_ref[pl.ds(n2, lines_out, stride=PITCH), :] = dot(
            table_ref[j], jnp.concatenate([high, high, rest], axis=0)
        )


def side_by_side(spec_ref, at):
    return jnp.concatenate([spec_ref[a, :] for a in at], axis=1)


def lines(spec_ref, n1, k1):
    at = [pl.multiple_of(p * PITCH, 8) for p in (k1, k1 + n1)]
    return [pl.ds(p, FINE) for p in at]


def filter_kernel(scale, filt_ref, first_ref, fine_ref, spread_ref, out_ref, wide_ref, space_ref, spec_ref):
    i = pl.program_id(0)
    n1 = space_ref.shape[0] // PITCH
    spots = spread_ref.shape[0]
    group = out_ref.shape[1]

    @pl.when(i == 0)
    def _():
        high, rest = split_value(filt_ref[...])
        short = filt_ref.shape[0]
        for j in range(spots):
            e = spread_ref[j]
            wide_ref[pl.ds(j, short, stride=spots), :] = scale * (dot(high, e) + dot(rest, e))
        for line in range(n1):
            space_ref[line * PITCH : line * PITCH + FINE, :] = wide_ref[line * FINE : (line + 1) * FINE, :]

    @pl.when(i < STEPS)
    def _():
        coarse(i, first_ref, space_ref, n1, spec_ref, 2 * n1)

    @pl.when(i >= STEPS)
    def _():
        for j in range(0, group, 2):
            at_re, at_im = zip(*(lines(spec_ref, n1, (i - STEPS) * group + j + e) for e in (0, 1)))
            z = fine(fine_ref, 0, side_by_side(spec_ref, at_re), side_by_side(spec_ref, at_im))
            for e in (0, 1):
                out_ref[0, j + e] = z[:FINE, e * FINE : (e + 1) * FINE]
                out_ref[1, j + e] = z[FINE:, e * FINE : (e + 1) * FINE]


def main_kernel(pair_ref, fspec_ref, first_ref, last_ref, fine_ref, out_ref, corr_ref, space_ref, spec_ref):
    i = pl.program_id(0)
    n1 = space_ref.shape[0] // PITCH
    group = fspec_ref.shape[1]

    @pl.when(i == 0)
    def _():
        for line in range(n1):
            space_ref[line * PITCH : line * PITCH + FINE, :] = pair_ref[line * FINE : (line + 1) * FINE, :]

    @pl.when(i < STEPS)
    def _():
        coarse(i, first_ref, space_ref, n1, spec_ref, 2 * n1)

    @pl.when((i >= STEPS) & (i < 2 * STEPS))
    def _():
        sign = jnp.where(low_lanes(FINE), 1.0, -1.0)
        for j in range(0, group, 2):
            at_re, at_im = zip(*(lines(spec_ref, n1, (i - STEPS) * group + j + e) for e in (0, 1)))
            z = fine(fine_ref, 0, side_by_side(spec_ref, at_re), side_by_side(spec_ref, at_im))
            prod = []
            for e in (0, 1):
                pr, pi = (z[p * FINE : (p + 1) * FINE, e * FINE : (e + 1) * FINE] for p in (0, 1))
                fr, fi = fspec_ref[0, j + e], fspec_ref[1, j + e] * sign
                qr, qi = pltpu.roll(pr, FINE // 2, 1), pltpu.roll(pi, FINE // 2, 1)
                corr_ref[0, j + e] = pr * qr + pi * qi
                corr_ref[1, j + e] = pr * qi - pi * qr
                prod.append((fr * pr - fi * pi, fr * pi + fi * pr))
            w = fine(fine_ref, 1, *(jnp.concatenate(part, axis=1) for part in zip(*prod)))
            for e in (0, 1):
                spec_ref[at_re[e], :] = w[:FINE, e * FINE : (e + 1) * FINE]
                spec_ref[at_im[e], :] = w[FINE:, e * FINE : (e + 1) * FINE]

    @pl.when(i >= 2 * STEPS)
    def _():
        coarse(i - 2 * STEPS, last_ref, spec_ref, 2 * n1, space_ref, n1)

    @pl.when(i == 3 * STEPS - 1)
    def _():
        for line in range(n1):
            out_ref[line * FINE : (line + 1) * FINE, :] = space_ref[line * PITCH : line * PITCH + FINE, :]


def lags_kernel(corr_ref, last_ref, fine_ref, fold_ref, lags_ref, wide_ref, space_ref, spec_ref):
    i = pl.program_id(0)
    n1 = space_ref.shape[0] // PITCH
    spots = fold_ref.shape[0]
    group = corr_ref.shape[1]

    @pl.when(i < STEPS)
    def _():
        for j in range(0, group, 2):
            at_re, at_im = zip(*(lines(spec_ref, n1, i * group + j + e) for e in (0, 1)))
            w = fine(
                fine_ref, 1, *(jnp.concatenate([corr_ref[p, j], corr_ref[p, j + 1]], axis=1) for p in (0, 1))
            )
            for e in (0, 1):
                spec_ref[at_re[e], :] = w[:FINE, e * FINE : (e + 1) * FINE]
                spec_ref[at_im[e], :] = w[FINE:, e * FINE : (e + 1) * FINE]

    @pl.when(i >= STEPS)
    def _():
        coarse(i - STEPS, last_ref, spec_ref, 2 * n1, space_ref, n1)

    @pl.when(i == 2 * STEPS - 1)
    def _():
        for line in range(n1):
            wide_ref[line * FINE : (line + 1) * FINE, :] = space_ref[line * PITCH : line * PITCH + FINE, :]
        short = lags_ref.shape[0]
        total = jnp.zeros((short, FINE), jnp.float32)
        for j in range(spots):
            high, rest = split_value(wide_ref[pl.ds(j, short, stride=spots), :])
            total += dot(high, fold_ref[j]) + dot(rest, fold_ref[j])
        lags_ref[...] = total


VMEM_BYTES = 60 << 20


def pack(k_gate, values, grad_out, q_gate, shards, table):
    rows, width = k_gate.shape
    tile = 128
    block = pl.BlockSpec((tile, width), lambda i: (i, 0))
    return pl.pallas_call(
        pack_kernel,
        grid=(rows // tile,),
        in_specs=[block] * 4 + [pl.BlockSpec((width, width), lambda i: (0, 0))],
        out_specs=pl.BlockSpec((shards, tile, FINE), lambda i: (0, i, 0)),
        out_shape=jax.ShapeDtypeStruct((shards, rows, FINE), jnp.float32),
        compiler_params=pltpu.CompilerParams(vmem_limit_bytes=VMEM_BYTES),
        cost_estimate=pl.CostEstimate(
            flops=8 * rows * width * width, bytes_accessed=24 * rows * width, transcendentals=0
        ),
        name="pack",
    )(k_gate, values, grad_out, q_gate, table)


def unpack(back, k_gate, values, grad_out, table):
    rows, width = k_gate.shape
    tile = 128
    block = pl.BlockSpec((tile, width), lambda i: (i, 0))
    return pl.pallas_call(
        unpack_kernel,
        grid=(rows // tile,),
        in_specs=[pl.BlockSpec((back.shape[0], tile, FINE), lambda i: (0, i, 0))]
        + [block] * 3
        + [pl.BlockSpec((width, width), lambda i: (0, 0))],
        out_specs=[block] * 3,
        out_shape=[jax.ShapeDtypeStruct((rows, width), jnp.float32)] * 3,
        compiler_params=pltpu.CompilerParams(vmem_limit_bytes=VMEM_BYTES),
        cost_estimate=pl.CostEstimate(
            flops=8 * rows * width * width, bytes_accessed=32 * rows * width, transcendentals=0
        ),
        name="unpack",
    )(back, k_gate, values, grad_out, table)


def whole(array):
    return pl.BlockSpec(array.shape, lambda i: (0,) * len(array.shape))


def phase(array, axis, start):
    block = tuple(d // STEPS if a == axis else d for a, d in enumerate(array.shape))

    def index(i):
        at = jnp.clip(i - start, 0, STEPS - 1)
        return tuple(at if a == axis else 0 for a in range(len(block)))

    return pl.BlockSpec(block, index)


def stepped(kernel, phases, ins, in_specs, outs, out_specs, scratch, flops, name):
    return pl.pallas_call(
        kernel,
        grid=(phases * STEPS,),
        in_specs=in_specs,
        out_specs=out_specs,
        out_shape=outs,
        scratch_shapes=[pltpu.VMEM((rows, FINE), jnp.float32) for rows in scratch],
        compiler_params=pltpu.CompilerParams(vmem_limit_bytes=VMEM_BYTES),
        cost_estimate=pl.CostEstimate(
            flops=flops, bytes_accessed=24 << 20, transcendentals=0
        ),
        name=name,
    )(*ins)


def spectral(length, own, chans):
    n1 = length // FINE
    first, last, mats = (jnp.asarray(t) for t in kernel_tables(length))
    spread, fold = (jnp.asarray(t) for t in fold_tables(own, chans))
    spec = jax.ShapeDtypeStruct((2, n1, FINE, FINE), jnp.float32)
    space = jax.ShapeDtypeStruct((length, FINE), jnp.float32)
    packed = jax.ShapeDtypeStruct((length * own // FINE, FINE), jnp.float32)
    padded = [n1 * PITCH, 2 * n1 * PITCH]

    def filter_stage(filt):
        return stepped(
            functools.partial(filter_kernel, float(length) ** -0.5), 2, (filt, first, mats, spread),
            [whole(filt), phase(first, 0, 0), whole(mats), whole(spread)],
            spec, phase(spec, 1, STEPS), [length] + padded, 15_000_000_000, "filter_spectrum",
        )

    def main_stage(pair, fspec):
        return stepped(
            main_kernel, 3, (pair, fspec, first, last, mats),
            [whole(pair), phase(fspec, 1, STEPS), phase(first, 0, 0), phase(last, 0, 2 * STEPS), whole(mats)],
            [space, spec], [whole(space), phase(spec, 1, STEPS)], padded, 30_000_000_000, "pair_stage",
        )

    def lags_stage(corr):
        return stepped(
            lags_kernel, 2, (corr, last, mats, fold),
            [phase(corr, 1, 0), phase(last, 0, STEPS), whole(mats), whole(fold)],
            packed, whole(packed), [length] + padded, 15_000_000_000, "lags",
        )

    return filter_stage, main_stage, lags_stage


def local(q_gate, k_gate, values, filter_raw, grad_out):
    rows, width = q_gate.shape
    nfilt = filter_raw.shape[1]
    shards = lax.axis_size("seq")
    length = rows * shards
    repeats = width // nfilt
    own = nfilt // shards
    chans = repeats * own
    scale = float(length) ** (-0.5)
    n1 = length // FINE
    first, last, tw_cos, tw_sin, ahead, back = tables(length)
    tw_cos = tw_cos[None, :, :, None][0]
    tw_sin = tw_sin[None, :, :, None][0]

    def split(block):
        groups = block.shape[1] // nfilt
        parts = block.reshape(rows, groups, shards, own)
        return parts.transpose(2, 0, 1, 3).reshape(shards, rows, groups * own)

    def merge(parts):
        groups = parts.shape[2] // own
        block = parts.reshape(shards, rows, groups, own).transpose(1, 2, 0, 3)
        return block.reshape(rows, groups * nfilt)

    def exchange(parts):
        return lax.all_to_all(parts, "seq", split_axis=0, concat_axis=0, tiled=True)

    if 2 * chans == FINE and n1 == 64:
        table = order_table(width, nfilt, own)
        filt = exchange(split(filter_raw).reshape(shards, -1, FINE))
        packed = pack(k_gate, values, grad_out, q_gate, shards, jnp.asarray(table))
        filt, packed = lax.optimization_barrier((filt, packed))
        pair = exchange(packed)
        filter_stage, main_stage, lags_stage = spectral(length, own, chans)
        fspec = filter_stage(filt.reshape(-1, FINE))
        out, corr = main_stage(pair.reshape(length, FINE), fspec)
        out = exchange(out.reshape(shards, rows, FINE))
        lags = lax.psum(lags_stage(corr), "chan") * scale
        grads = unpack(out, k_gate, values, grad_out, jnp.asarray(table.T))
        lags, _ = lax.optimization_barrier((lags, grads[0]))
        lags = merge(exchange(lags.reshape(shards, -1, FINE)).reshape(shards, rows, own))
        return tuple(grads) + (lags,)

    def forward(block):
        wide = block.shape[1]
        part = mul("pkn,nbw->pkbw", first, block.reshape(n1, FINE, wide))
        real, imag = part[0], part[1]
        turned = jnp.stack([real * tw_cos + imag * tw_sin, imag * tw_cos - real * tw_sin])
        return mul("opkn,ptnw->otkw", ahead, turned)

    def inverse(spec):
        wide = spec.shape[3]
        part = mul("opkn,ptnw->otkw", back, spec)
        real, imag = part[0], part[1]
        turned = jnp.stack([real * tw_cos - imag * tw_sin, imag * tw_cos + real * tw_sin])
        return mul("pkn,pkbw->nbw", last, turned).reshape(length, wide)

    pair = jnp.concatenate([split(k_gate * values), split(grad_out * q_gate)], axis=2)
    pair = exchange(pair).reshape(length, 2 * chans)
    filt = split(filter_raw * scale).reshape(shards, -1, FINE)
    filt = exchange(filt).reshape(length, own)

    spec = forward(pair)
    gr, gi = spec[0, :, :, :chans], spec[1, :, :, :chans]
    qr, qi = spec[0, :, :, chans:], spec[1, :, :, chans:]
    fspec = jnp.tile(forward(filt), (1, 1, 1, repeats))
    fr, fi = fspec[0], fspec[1]
    conv = jnp.stack([fr * gr - fi * gi, fr * gi + fi * gr])
    adj = jnp.stack([fr * qr + fi * qi, fr * qi - fi * qr])
    corr = jnp.stack([gr * qr + gi * qi, gr * qi - gi * qr])
    corr = corr.reshape(2, n1, FINE, repeats, own).sum(axis=3)
    out = inverse(jnp.concatenate([conv, adj], axis=3)).reshape(shards, rows, 2 * chans)
    lags = inverse(corr).reshape(shards, -1, FINE)
    out = exchange(out)
    lags = exchange(lax.psum(lags, "chan") * scale).reshape(shards, rows, own)

    grad_gated = merge(out[:, :, chans:])
    return (
        grad_out * merge(out[:, :, :chans]),
        grad_gated * values,
        grad_gated * k_gate,
        merge(lags),
    )


def solution(mesh):
    placed = P("seq", "chan")
    return jax.shard_map(
        local,
        mesh=mesh,
        in_specs=(placed, placed, placed, P("seq", None), placed),
        out_specs=(placed, placed, placed, P("seq", None)),
        check_vma=False,
    )
```
